32 devices in a mesh: flow: 16 (over z, y, x), lat: 2 (over core).
Axes of the slice: x: 2, y: 2, z: 4, core: 2. Of those that a mesh axis runs over, the one named last changes fastest.
Arguments:
- concentration: float32 [3, 256, 64, 128], P(None, 'flow', 'lat'), may hold values from 0 to 2
- courant: float32 [3, 256, 64, 128], P(None, 'flow', 'lat'), may hold values from 500 to 4000
- rates: float32 [2, 256, 64, 128], P(None, 'flow', 'lat'), may hold values from 0.2 to 3
- spread: float32 [64, 128], P('lat'), may hold values from 0.02 to 0.2
- inlet: float32 [3, 64, 128], P(None, 'lat'), may hold values from 200 to 2000
Outputs:
- fresh: float32 [3, 256, 64, 128], P(None, 'flow', 'lat')
The draws below stay inside these ranges and needn't reach their ends.
All inputs are finite; a program needn't handle non-finite values.
Results may differ from the reference program's by a relative error of at most 0.000066.
Values sent between devices are 32-bit elements; how exact they have to be, the bound alone decides.
A program may use at most 64 MiB of HBM per device.

```python
import math
import jax
import jax.numpy as jnp
from jax import lax

NZ = 128
NX = 256
NY = 64


def block_scale(own_key, extent, pieces, low, top_value):
    def one(dim, blocks):
        heights = jax.random.uniform(jax.random.fold_in(jax.random.fold_in(own_key, 6), dim), (blocks,), jnp.float32, low / len(pieces), top_value / len(pieces))
        return jnp.repeat(jnp.exp(heights), extent[dim] // blocks).reshape((-1,) + (1,) * (len(extent) - dim - 1))

    loudness = one(*pieces[0])
    for cut in pieces[1:]:
        loudness = loudness * one(*cut)
    return loudness


def setup_inputs(seed: int = 0) -> dict:
    streams_of = jax.random.split(jax.random.key(seed), 6)
    return {
        "concentration": jnp.clip(2.0 * jax.random.uniform(streams_of[0], (3, NX, NY, NZ), jnp.float32) ** block_scale(streams_of[0], (3, NX, NY, NZ), ((1, 16), (2, 2)), -0.2, 0.2), 0.0, 2.0),
        "courant": jnp.clip(jnp.exp(math.log(4000.0) - 2.0794415 * jax.random.uniform(streams_of[1], (3, NX, NY, NZ), jnp.float32) ** block_scale(streams_of[1], (3, NX, NY, NZ), ((1, 16), (2, 2)), -0.2, 0.2)), 500.0, 4000.0),
        "rates": jnp.clip(jnp.exp(math.log(3.0) - 2.7080502 * jax.random.uniform(streams_of[2], (2, NX, NY, NZ), jnp.float32) ** block_scale(streams_of[2], (2, NX, NY, NZ), ((1, 16), (2, 2)), -0.2, 0.2)), 0.2, 3.0),
        "spread": jnp.clip(jnp.exp(math.log(0.2) - 2.3025851 * jax.random.uniform(streams_of[3], (NY, NZ), jnp.float32) ** block_scale(streams_of[3], (NY, NZ), ((0, 2),), -0.2, 0.2)), 0.02, 0.2),
        "inlet": jnp.clip(jnp.exp(math.log(2000.0) - 2.3025851 * jax.random.uniform(streams_of[4], (3, NY, NZ), jnp.float32) ** block_scale(streams_of[4], (3, NY, NZ), ((1, 2),), -0.2, 0.2)), 200.0, 2000.0),
    }


def lateral(concentration, spread):
    padded = jnp.pad(concentration, ((0, 0), (0, 0), (1, 1), (1, 1)))
    beside = padded[:, :, 2:, 1:-1] + padded[:, :, :-2, 1:-1]
    beside = beside + padded[:, :, 1:-1, 2:] + padded[:, :, 1:-1, :-2]
    return concentration + spread[None, None] * (beside - 4.0 * concentration)


def reference(concentration, courant, rates, spread, inlet):
    source = lateral(concentration, spread)

    def advance(flux, cell):
        src, cour, rate = cell
        first = (src[0] + flux[0]) / (1.0 + cour[0] + rate[0])
        second = (src[1] + flux[1] + rate[0] * first) / (1.0 + cour[1] + rate[1])
        third = (src[2] + flux[2] + rate[1] * second) / (1.0 + cour[2])
        fresh_cell = jnp.stack([first, second, third])
        return cour * fresh_cell, fresh_cell

    cells = (jnp.moveaxis(source, 1, 0), jnp.moveaxis(courant, 1, 0), jnp.moveaxis(rates, 1, 0))
    _, result = lax.scan(advance, inlet, cells)
    return jnp.moveaxis(result, 0, 1)
```

```python
import functools
import jax
import jax.numpy as jnp
from jax import lax
from jax.experimental import pallas as pl
from jax.experimental.pallas import tpu as pltpu
from jax.sharding import PartitionSpec as P

MESH = pl.DeviceIdType.MESH
GROUP = 4
EDGE = 8


def apply_map(m, q):
    return (
        m[0] * q[0] + m[6],
        m[1] * q[0] + m[2] * q[1] + m[7],
        m[3] * q[0] + m[4] * q[1] + m[5] * q[2] + m[8],
    )


def after(m, n):
    lower = (
        m[0] * n[0],
        m[1] * n[0] + m[2] * n[1],
        m[2] * n[2],
        m[3] * n[0] + m[4] * n[1] + m[5] * n[3],
        m[4] * n[2] + m[5] * n[4],
        m[5] * n[5],
    )
    return lower + apply_map(m, n[6:])


def kernel(
    groups, group, lats,
    conc, courant, rates, spread, inlet, out,
    pad, cour, rate, spr, inl, local, mine, maps, total, totals, fluxes, entering,
    load_sem, halo_send, halo_recv, a_send, a_recv, b_send, b_recv, c_send, c_recv,
):
    cells, rows, width = cour.shape[1:]
    part = rows // group
    flow = lax.axis_index("flow")
    lat = lax.axis_index("lat")
    inner = lax.rem(flow, group)
    outer = lax.div(flow, group)

    loads = [
        pltpu.make_async_copy(src, dst, load_sem.at[i])
        for i, (src, dst) in enumerate((
            (courant, cour), (rates, rate), (conc, pad.at[:, :, EDGE:EDGE + rows]),
            (spread, spr), (inlet, inl),
        ))
    ]
    for load in loads:
        load.start()

    barrier = pltpu.get_barrier_semaphore()
    for step in range(1, group):
        peer = outer * group + lax.rem(inner + step, group)
        pl.semaphore_signal(barrier, inc=1, device_id={"flow": peer}, device_id_type=MESH)
    for step in range(1, groups):
        peer = lax.rem(outer + step, groups) * group + inner
        pl.semaphore_signal(barrier, inc=1, device_id={"flow": peer}, device_id_type=MESH)

    @pl.when(lat > 0)
    def _():
        pl.semaphore_signal(barrier, inc=1, device_id={"lat": lat - 1}, device_id_type=MESH)

    @pl.when(lat < lats - 1)
    def _():
        pl.semaphore_signal(barrier, inc=1, device_id={"lat": lat + 1}, device_id_type=MESH)

    beside = jnp.where(lat > 0, 1, 0) + jnp.where(lat < lats - 1, 1, 0)
    pl.semaphore_wait(barrier, group - 1 + groups - 1 + beside)

    to_high = pltpu.make_async_remote_copy(
        src_ref=conc.at[:, :, rows - EDGE:rows], dst_ref=pad.at[:, :, 0:EDGE],
        send_sem=halo_send.at[0], recv_sem=halo_recv.at[0],
        device_id={"lat": lat + 1}, device_id_type=MESH,
    )
    to_low = pltpu.make_async_remote_copy(
        src_ref=conc.at[:, :, 0:EDGE], dst_ref=pad.at[:, :, EDGE + rows:2 * EDGE + rows],
        send_sem=halo_send.at[1], recv_sem=halo_recv.at[1],
        device_id={"lat": lat - 1}, device_id_type=MESH,
    )
    nothing = jnp.zeros((3, cells, EDGE, width), jnp.float32)

    @pl.when(lat < lats - 1)
    def _():
        to_high.start()

    @pl.when(lat > 0)
    def _():
        to_low.start()

    @pl.when(lat == 0)
    def _():
        pad[:, :, 0:EDGE] = nothing

    @pl.when(lat == lats - 1)
    def _():
        pad[:, :, EDGE + rows:2 * EDGE + rows] = nothing

    for load in loads:
        load.wait()

    @pl.when(lat > 0)
    def _():
        to_high.wait_recv()

    @pl.when(lat < lats - 1)
    def _():
        to_low.wait_recv()

    scale = spr[...]
    lane = lax.broadcasted_iota(jnp.int32, (rows, width), 1)
    first, last = lane == 0, lane == width - 1

    def source(k, i):
        mid = pad[k, i, EDGE:EDGE + rows]
        left = jnp.where(first, 0.0, pltpu.roll(mid, 1, 1))
        right = jnp.where(last, 0.0, pltpu.roll(mid, width - 1, 1))
        near = pad[k, i, EDGE - 1:EDGE - 1 + rows] + pad[k, i, EDGE + 1:EDGE + 1 + rows]
        return mid + scale * (near + left + right - 4.0 * mid)

    def cell(i, state):
        m00, m10, m11, m20, m21, m22, w0, w1, w2 = state
        c0, c1, c2 = cour[0, i], cour[1, i], cour[2, i]
        k0, k1 = rate[0, i], rate[1, i]
        r0, r1, r2 = 1.0 / (1.0 + c0 + k0), 1.0 / (1.0 + c1 + k1), 1.0 / (1.0 + c2)
        u00 = m00 * r0
        u10 = (m10 + k0 * u00) * r1
        u20 = (m20 + k1 * u10) * r2
        u11 = m11 * r1
        u21 = (m21 + k1 * u11) * r2
        u22 = m22 * r2
        v0 = (source(0, i) + w0) * r0
        v1 = (source(1, i) + w1 + k0 * v0) * r1
        v2 = (source(2, i) + w2 + k1 * v1) * r2
        values = (u00, u10, u11, u20, u21, u22, v0, v1, v2)
        for q, value in enumerate(values):
            local[q, i] = value
        factors = (c0, c1, c1, c2, c2, c2, c0, c1, c2)
        return tuple(f * v for f, v in zip(factors, values))

    one = jnp.ones((rows, width), jnp.float32)
    zero = jnp.zeros((rows, width), jnp.float32)
    state = lax.fori_loop(
        0, cells, cell, (one, zero, one, zero, zero, one, zero, zero, zero)
    )
    for g in range(group):
        for q in range(9):
            mine[g, q] = state[q][g * part:(g + 1) * part]

    def to_owner(step):
        peer = lax.rem(inner + step, group)
        return pltpu.make_async_remote_copy(
            src_ref=mine.at[peer], dst_ref=maps.at[inner],
            send_sem=a_send.at[peer], recv_sem=a_recv.at[inner],
            device_id={"flow": outer * group + peer}, device_id_type=MESH,
        )

    def from_member(step):
        peer = lax.rem(inner + step, group)
        return pltpu.make_async_remote_copy(
            src_ref=mine.at[peer], dst_ref=maps.at[peer],
            send_sem=a_send.at[peer], recv_sem=a_recv.at[peer],
            device_id={"flow": outer * group + peer}, device_id_type=MESH,
        )

    for step in range(1, group):
        to_owner(step).start()
    maps[inner] = mine[inner]
    for step in range(1, group):
        from_member(step).wait_recv()

    def map_of(ref, m):
        return tuple(ref[m, q] for q in range(9))

    flux = tuple(inl[k, pl.ds(pl.multiple_of(inner * part, part), part)] for k in range(3))

    def to_group(o):
        return pltpu.make_async_remote_copy(
            src_ref=total, dst_ref=totals.at[outer],
            send_sem=b_send.at[o], recv_sem=b_recv.at[outer],
            device_id={"flow": o * group + inner}, device_id_type=MESH,
        )

    if groups > 1:
        product = map_of(maps, 0)
        for m in range(1, group):
            product = after(map_of(maps, m), product)
        for q in range(9):
            total[q] = product[q]

        for o in range(1, groups):
            @pl.when(outer < o)
            def _():
                to_group(o).start()

        def earlier(o, flux):
            pltpu.make_async_remote_copy(
                src_ref=total, dst_ref=totals.at[o],
                send_sem=b_send.at[o], recv_sem=b_recv.at[o],
                device_id={"flow": o * group + inner}, device_id_type=MESH,
            ).wait_recv()
            return apply_map(map_of(totals, o), flux)

        flux = lax.fori_loop(0, outer, earlier, flux)

    for m in range(group):
        for k in range(3):
            fluxes[m, k] = flux[k]
        if m < group - 1:
            flux = apply_map(map_of(maps, m), flux)

    def to_member(step):
        peer = lax.rem(inner + step, group)
        return pltpu.make_async_remote_copy(
            src_ref=fluxes.at[peer], dst_ref=entering.at[inner],
            send_sem=c_send.at[peer], recv_sem=c_recv.at[inner],
            device_id={"flow": outer * group + peer}, device_id_type=MESH,
        )

    def from_owner(step):
        peer = lax.rem(inner + step, group)
        return pltpu.make_async_remote_copy(
            src_ref=fluxes.at[peer], dst_ref=entering.at[peer],
            send_sem=c_send.at[peer], recv_sem=c_recv.at[peer],
            device_id={"flow": outer * group + peer}, device_id_type=MESH,
        )

    for step in range(1, group):
        to_member(step).start()
    entering[inner] = fluxes[inner]
    for step in range(1, group):
        from_owner(step).wait_recv()

    q = [jnp.concatenate([entering[g, k] for g in range(group)], axis=0) for k in range(3)]

    def finish(i, carry):
        fresh = apply_map(tuple(local[n, i] for n in range(9)), q)
        for k in range(3):
            out[k, i] = fresh[k]
        return carry

    lax.fori_loop(0, cells, finish, 0)

    for step in range(1, group):
        to_owner(step).wait_send()
        to_member(step).wait_send()
    for o in range(1, groups):
        @pl.when(outer < o)
        def _():
            to_group(o).wait_send()

    @pl.when(lat < lats - 1)
    def _():
        to_high.wait_send()

    @pl.when(lat > 0)
    def _():
        to_low.wait_send()


def per_device(flows, lats, concentration, courant, rates, spread, inlet):
    _, cells, rows, width = concentration.shape
    group = GROUP
    groups = flows // group
    part = rows // group
    f32 = jnp.float32
    dma = pltpu.SemaphoreType.DMA
    return pl.pallas_call(
        functools.partial(kernel, groups, group, lats),
        out_shape=jax.ShapeDtypeStruct(concentration.shape, f32),
        in_specs=[pl.BlockSpec(memory_space=pltpu.HBM)] * 5,
        out_specs=pl.BlockSpec(memory_space=pltpu.VMEM),
        scratch_shapes=[
            pltpu.VMEM((3, cells, rows + 2 * EDGE, width), f32),
            pltpu.VMEM((3, cells, rows, width), f32),
            pltpu.VMEM((2, cells, rows, width), f32),
            pltpu.VMEM((rows, width), f32),
            pltpu.VMEM((3, rows, width), f32),
            pltpu.VMEM((9, cells, rows, width), f32),
            pltpu.VMEM((group, 9, part, width), f32),
            pltpu.VMEM((group, 9, part, width), f32),
            pltpu.VMEM((9, part, width), f32),
            pltpu.VMEM((groups, 9, part, width), f32),
            pltpu.VMEM((group, 3, part, width), f32),
            pltpu.VMEM((group, 3, part, width), f32),
            dma((5,)), dma((2,)), dma((2,)),
            dma((group,)), dma((group,)),
            dma((groups,)), dma((groups,)),
            dma((group,)), dma((group,)),
        ],
        compiler_params=pltpu.CompilerParams(
            collective_id=0, has_side_effects=True, vmem_limit_bytes=24 * 2**20
        ),
        cost_estimate=pl.CostEstimate(
            flops=100 * cells * rows * width, bytes_accessed=44 * cells * rows * width,
            transcendentals=0,
        ),
    )(concentration, courant, rates, spread, inlet)


def solution(mesh):
    in_specs = (
        P(None, "flow", "lat", None),
        P(None, "flow", "lat", None),
        P(None, "flow", "lat", None),
        P("lat", None),
        P(None, "lat", None),
    )
    out_specs = P(None, "flow", "lat", None)
    body = functools.partial(per_device, mesh.shape["flow"], mesh.shape["lat"])
    return jax.shard_map(
        body, mesh=mesh, in_specs=in_specs, out_specs=out_specs, check_vma=False
    )
```

```python
import functools
import jax
import jax.numpy as jnp
from jax import lax
from jax.experimental import pallas as pl
from jax.experimental.pallas import tpu as pltpu
from jax.sharding import PartitionSpec as P

MESH = pl.DeviceIdType.MESH
GROUP = 4
EDGE = 8
UNROLL = 16


def apply_map(m, q):
    return (
        m[0] * q[0] + m[6],
        m[1] * q[0] + m[2] * q[1] + m[7],
        m[3] * q[0] + m[4] * q[1] + m[5] * q[2] + m[8],
    )


def times(m, n):
    return (
        m[0] * n[0],
        m[1] * n[0] + m[2] * n[1],
        m[2] * n[2],
        m[3] * n[0] + m[4] * n[1] + m[5] * n[3],
        m[4] * n[2] + m[5] * n[4],
        m[5] * n[5],
    )


def inverse(x):
    rough = pl.reciprocal(x, approx=True)
    return rough * (2.0 - x * rough)


def kernel(
    groups, group, lats,
    conc, courant, rates, spread, inlet, out,
    pad, cour, rate, spr, inl, local, inv, mine, maps, total, totals, fluxes, entering,
    load_sem, tile_sem, halo_send, halo_recv,
    a_send, a_recv, o_send, o_recv, b_send, b_recv, p_send, p_recv, c_send, c_recv,
):
    cells, rows, width = cour.shape[1:]
    part = rows // group
    tile = max(part, EDGE)
    owners = tile // part
    tiles = rows // tile
    flow = lax.axis_index("flow")
    lat = lax.axis_index("lat")
    inner = lax.rem(flow, group)
    outer = lax.div(flow, group)
    not_low, not_high = lat > 0, lat < lats - 1

    def tile_at(step):
        return lax.rem(lax.div(inner, owners) + step, tiles)

    def rows_of(t):
        return pl.ds(pl.multiple_of(t * tile, tile), tile)

    order = [tile_at(step) for step in range(1, tiles)] + [tile_at(0)]
    tile_loads = []
    for n, t in enumerate(order):
        at = rows_of(t)
        tile_loads.append([
            pltpu.make_async_copy(courant.at[:, :, at], cour.at[:, :, at], tile_sem.at[0, n]),
            pltpu.make_async_copy(rates.at[:, :, at], rate.at[:, :, at], tile_sem.at[1, n]),
        ])
    loads = [
        pltpu.make_async_copy(src, dst, load_sem.at[i])
        for i, (src, dst) in enumerate((
            (conc, pad.at[:, :, EDGE:EDGE + rows]), (spread, spr), (inlet, inl),
        ))
    ]
    for load in sum(tile_loads, []) + loads:
        load.start()

    barrier = pltpu.get_barrier_semaphore()
    for step in range(1, group):
        peer = outer * group + lax.rem(inner + step, group)
        pl.semaphore_signal(barrier, inc=1, device_id={"flow": peer}, device_id_type=MESH)
    for step in range(1, groups):
        peer = lax.rem(outer + step, groups) * group + inner
        pl.semaphore_signal(barrier, inc=1, device_id={"flow": peer}, device_id_type=MESH)

    @pl.when(not_low)
    def _():
        pl.semaphore_signal(barrier, inc=1, device_id={"lat": lat - 1}, device_id_type=MESH)

    @pl.when(not_high)
    def _():
        pl.semaphore_signal(barrier, inc=1, device_id={"lat": lat + 1}, device_id_type=MESH)

    nothing = jnp.zeros((3, cells, EDGE, width), jnp.float32)

    @pl.when(lat == 0)
    def _():
        pad[:, :, 0:EDGE] = nothing

    @pl.when(lat == lats - 1)
    def _():
        pad[:, :, EDGE + rows:2 * EDGE + rows] = nothing

    beside = jnp.where(not_low, 1, 0) + jnp.where(not_high, 1, 0)
    pl.semaphore_wait(barrier, group - 1 + groups - 1 + beside)

    to_high = pltpu.make_async_remote_copy(
        src_ref=conc.at[:, :, rows - EDGE:rows], dst_ref=pad.at[:, :, 0:EDGE],
        send_sem=halo_send.at[0], recv_sem=halo_recv.at[0],
        device_id={"lat": lat + 1}, device_id_type=MESH,
    )
    to_low = pltpu.make_async_remote_copy(
        src_ref=conc.at[:, :, 0:EDGE], dst_ref=pad.at[:, :, EDGE + rows:2 * EDGE + rows],
        send_sem=halo_send.at[1], recv_sem=halo_recv.at[1],
        device_id={"lat": lat - 1}, device_id_type=MESH,
    )

    @pl.when(not_high)
    def _():
        to_high.start()

    @pl.when(not_low)
    def _():
        to_low.start()

    matrix, offset = slice(0, 6), slice(6, 9)

    def between(src, dst, there, send, recv, slot, cut, peer, arriving):
        lands = peer if arriving else slot
        return pltpu.make_async_remote_copy(
            src_ref=src.at[peer, cut], dst_ref=dst.at[lands, cut],
            send_sem=send.at[peer], recv_sem=recv.at[lands],
            device_id={"flow": there(peer)}, device_id_type=MESH,
        )

    def member(peer):
        return outer * group + peer

    def matrix_copy(peer, arriving=False):
        return between(mine, maps, member, a_send, a_recv, inner, matrix, peer, arriving)

    def offset_copy(peer, arriving=False):
        return between(mine, maps, member, o_send, o_recv, inner, offset, peer, arriving)

    def flux_copy(peer, arriving=False):
        return between(fluxes, entering, member, c_send, c_recv, inner, slice(0, 3), peer, arriving)

    def put(t, last, values, first, copy):
        for j in range(owners):
            peer = t * owners + j
            for q, value in enumerate(values):
                mine[peer, first + q] = value[j * part:(j + 1) * part]
            if last:
                @pl.when(peer != inner)
                def _():
                    copy(peer).start()
            else:
                copy(peer).start()

    one = jnp.ones((tile, width), jnp.float32)
    zero = jnp.zeros((tile, width), jnp.float32)

    for n, t in enumerate(order):
        for load in tile_loads[n]:
            load.wait()
        at = rows_of(t)

        def matrix_cell(i, state, at=at):
            m00, m10, m11, m20, m21, m22 = state
            c0, c1, c2 = cour[0, i, at], cour[1, i, at], cour[2, i, at]
            k0, k1 = rate[0, i, at], rate[1, i, at]
            r0, r1, r2 = inverse(1.0 + c0 + k0), inverse(1.0 + c1 + k1), inverse(1.0 + c2)
            for k, r in enumerate((r0, r1, r2)):
                inv[k, i, at] = r
            u00 = m00 * r0
            u10 = (m10 + k0 * u00) * r1
            u20 = (m20 + k1 * u10) * r2
            u11 = m11 * r1
            u21 = (m21 + k1 * u11) * r2
            u22 = m22 * r2
            for q, value in enumerate((u00, u10, u11, u20, u21, u22)):
                local[q, i, at] = value
            return c0 * u00, c1 * u10, c1 * u11, c2 * u20, c2 * u21, c2 * u22

        state = lax.fori_loop(
            0, cells, matrix_cell, (one, zero, one, zero, zero, one), unroll=UNROLL
        )
        put(t, n == tiles - 1, state, 0, matrix_copy)

    for load in loads:
        load.wait()

    @pl.when(not_low)
    def _():
        to_high.wait_recv()

    @pl.when(not_high)
    def _():
        to_low.wait_recv()

    lane = lax.broadcasted_iota(jnp.int32, (tile, width), 1)
    first, last = lane == 0, lane == width - 1

    for n, t in enumerate(order):
        at = rows_of(t)
        scale = spr[at]

        def source(k, i, t=t, scale=scale):
            mid = pad[k, i, pl.ds(pl.multiple_of(t * tile + EDGE, EDGE), tile)]
            left = jnp.where(first, 0.0, pltpu.roll(mid, 1, 1))
            right = jnp.where(last, 0.0, pltpu.roll(mid, width - 1, 1))
            up = pad[k, i, pl.ds(t * tile + EDGE - 1, tile)]
            down = pad[k, i, pl.ds(t * tile + EDGE + 1, tile)]
            return mid + scale * (up + down + left + right - 4.0 * mid)

        def offset_cell(i, state, at=at, source=source):
            w0, w1, w2 = state
            v0 = (source(0, i) + w0) * inv[0, i, at]
            v1 = (source(1, i) + w1 + rate[0, i, at] * v0) * inv[1, i, at]
            v2 = (source(2, i) + w2 + rate[1, i, at] * v1) * inv[2, i, at]
            for k, value in enumerate((v0, v1, v2)):
                local[6 + k, i, at] = value
            return cour[0, i, at] * v0, cour[1, i, at] * v1, cour[2, i, at] * v2

        state = lax.fori_loop(0, cells, offset_cell, (zero, zero, zero), unroll=UNROLL)
        put(t, n == tiles - 1, state, 6, offset_copy)

    maps[inner] = mine[inner]

    def map_of(ref, m):
        return tuple(ref[m, q] for q in range(9))

    def group_copy(o, cut, send, recv, arriving):
        lands = o if arriving else outer
        return pltpu.make_async_remote_copy(
            src_ref=total.at[cut], dst_ref=totals.at[lands, cut],
            send_sem=send.at[o], recv_sem=recv.at[lands],
            device_id={"flow": o * group + inner}, device_id_type=MESH,
        )

    def total_matrix(o, arriving=False):
        return group_copy(o, matrix, b_send, b_recv, arriving)

    def total_offset(o, arriving=False):
        return group_copy(o, offset, p_send, p_recv, arriving)

    def to_later(copy):
        for o in reversed(range(1, groups)):
            @pl.when(outer < o)
            def _():
                copy(o).start()

    peers = [lax.rem(inner + step, group) for step in range(1, group)]
    for peer in peers:
        matrix_copy(peer, True).wait_recv()
    if groups > 1:
        product = tuple(maps[0, q] for q in range(6))
        for m in range(1, group):
            product = times(tuple(maps[m, q] for q in range(6)), product)
        for q in range(6):
            total[q] = product[q]
        to_later(total_matrix)
    for peer in peers:
        offset_copy(peer, True).wait_recv()

    flux = tuple(inl[k, pl.ds(pl.multiple_of(inner * part, part), part)] for k in range(3))
    if groups > 1:
        shift = tuple(maps[0, q] for q in range(6, 9))
        for m in range(1, group):
            shift = apply_map(map_of(maps, m), shift)
        for k in range(3):
            total[6 + k] = shift[k]
        to_later(total_offset)

        def earlier(o, flux):
            total_matrix(o, True).wait_recv()
            total_offset(o, True).wait_recv()
            return apply_map(map_of(totals, o), flux)

        flux = lax.fori_loop(0, outer, earlier, flux)

    for m in range(group):
        for k in range(3):
            fluxes[m, k] = flux[k]
        if m < group - 1:
            flux = apply_map(map_of(maps, m), flux)
    for peer in peers:
        flux_copy(peer).start()
    entering[inner] = fluxes[inner]

    for step in range(tiles):
        t = tile_at(step)
        at = rows_of(t)
        for j in range(owners):
            peer = t * owners + j
            if step:
                flux_copy(peer, True).wait_recv()
            else:
                @pl.when(peer != inner)
                def _():
                    flux_copy(peer, True).wait_recv()
        q = [
            jnp.concatenate([entering[t * owners + j, k] for j in range(owners)], axis=0)
            for k in range(3)
        ]

        def finish(i, carry, at=at, q=q):
            fresh = apply_map(tuple(local[n, i, at] for n in range(9)), q)
            for k in range(3):
                out[k, i, at] = fresh[k]
            return carry

        lax.fori_loop(0, cells, finish, 0, unroll=UNROLL)

    for peer in peers:
        matrix_copy(peer).wait_send()
        offset_copy(peer).wait_send()
        flux_copy(peer).wait_send()
    for o in range(1, groups):
        @pl.when(outer < o)
        def _():
            total_matrix(o).wait_send()
            total_offset(o).wait_send()

    @pl.when(not_high)
    def _():
        to_high.wait_send()

    @pl.when(not_low)
    def _():
        to_low.wait_send()


def per_device(flows, lats, concentration, courant, rates, spread, inlet):
    _, cells, rows, width = concentration.shape
    group = GROUP
    groups = flows // group
    part = rows // group
    f32 = jnp.float32
    dma = pltpu.SemaphoreType.DMA
    return pl.pallas_call(
        functools.partial(kernel, groups, group, lats),
        out_shape=jax.ShapeDtypeStruct(concentration.shape, f32),
        in_specs=[pl.BlockSpec(memory_space=pltpu.HBM)] * 5,
        out_specs=pl.BlockSpec(memory_space=pltpu.VMEM),
        scratch_shapes=[
            pltpu.VMEM((3, cells, rows + 2 * EDGE, width), f32),
            pltpu.VMEM((3, cells, rows, width), f32),
            pltpu.VMEM((2, cells, rows, width), f32),
            pltpu.VMEM((rows, width), f32),
            pltpu.VMEM((3, rows, width), f32),
            pltpu.VMEM((9, cells, rows, width), f32),
            pltpu.VMEM((3, cells, rows, width), f32),
            pltpu.VMEM((group, 9, part, width), f32),
            pltpu.VMEM((group, 9, part, width), f32),
            pltpu.VMEM((9, part, width), f32),
            pltpu.VMEM((groups, 9, part, width), f32),
            pltpu.VMEM((group, 3, part, width), f32),
            pltpu.VMEM((group, 3, part, width), f32),
            dma((3,)), dma((2, rows // max(part, EDGE))), dma((2,)), dma((2,)),
            dma((group,)), dma((group,)), dma((group,)), dma((group,)),
            dma((groups,)), dma((groups,)), dma((groups,)), dma((groups,)),
            dma((group,)), dma((group,)),
        ],
        compiler_params=pltpu.CompilerParams(
            collective_id=0, has_side_effects=True, vmem_limit_bytes=24 * 2**20
        ),
        cost_estimate=pl.CostEstimate(
            flops=100 * cells * rows * width, bytes_accessed=44 * cells * rows * width,
            transcendentals=0,
        ),
    )(*(
        pltpu.with_memory_space_constraint(array, pltpu.HBM)
        for array in (concentration, courant, rates, spread, inlet)
    ))


def solution(mesh):
    in_specs = (
        P(None, "flow", "lat", None),
        P(None, "flow", "lat", None),
        P(None, "flow", "lat", None),
        P("lat", None),
        P(None, "lat", None),
    )
    out_specs = P(None, "flow", "lat", None)
    body = functools.partial(per_device, mesh.shape["flow"], mesh.shape["lat"])
    return jax.shard_map(
        body, mesh=mesh, in_specs=in_specs, out_specs=out_specs, check_vma=False
    )
```

```python
import functools
import jax
import jax.numpy as jnp
from jax import lax
from jax.experimental import pallas as pl
from jax.experimental.pallas import tpu as pltpu
from jax.sharding import PartitionSpec as P

MESH = pl.DeviceIdType.MESH
GROUP = 4
EDGE = 8
UNROLL = 16


def apply_map(m, q):
    return (
        m[0] * q[0] + m[6],
        m[1] * q[0] + m[2] * q[1] + m[7],
        m[3] * q[0] + m[4] * q[1] + m[5] * q[2] + m[8],
    )


def times(m, n):
    return (
        m[0] * n[0],
        m[1] * n[0] + m[2] * n[1],
        m[2] * n[2],
        m[3] * n[0] + m[4] * n[1] + m[5] * n[3],
        m[4] * n[2] + m[5] * n[4],
        m[5] * n[5],
    )


def inverse(x):
    rough = pl.reciprocal(x, approx=True)
    return rough * (2.0 - x * rough)


def kernel(
    groups, group, lats,
    conc, courant, rates, spread, inlet, out,
    pad, cour, rate, spr, inl, local, inv, mine, maps, total, totals, fluxes, entering,
    load_sem, tile_sem, halo_send, halo_recv,
    a_send, a_recv, o_send, o_recv, b_send, b_recv, p_send, p_recv, c_send, c_recv,
):
    cells, rows, width = cour.shape[1:]
    part = rows // group
    tile = max(part, EDGE)
    owners = tile // part
    tiles = rows // tile
    flow = lax.axis_index("flow")
    lat = lax.axis_index("lat")
    inner = lax.rem(flow, group)
    outer = lax.div(flow, group)
    not_low, not_high = lat > 0, lat < lats - 1

    def tile_at(step):
        return lax.rem(lax.div(inner, owners) + step, tiles)

    def rows_of(t):
        return pl.ds(pl.multiple_of(t * tile, tile), tile)

    order = [tile_at(step) for step in range(1, tiles)] + [tile_at(0)]
    tile_loads = []
    for n, t in enumerate(order):
        at = rows_of(t)
        tile_loads.append([
            pltpu.make_async_copy(courant.at[:, :, at], cour.at[:, :, at], tile_sem.at[0, n]),
            pltpu.make_async_copy(rates.at[:, :, at], rate.at[:, :, at], tile_sem.at[1, n]),
        ])
    loads = [
        pltpu.make_async_copy(src, dst, load_sem.at[i])
        for i, (src, dst) in enumerate((
            (conc, pad.at[:, :, EDGE:EDGE + rows]), (spread, spr), (inlet, inl),
        ))
    ]
    barrier = pltpu.get_barrier_semaphore()
    for step in range(1, group):
        peer = outer * group + lax.rem(inner + step, group)
        pl.semaphore_signal(barrier, inc=1, device_id={"flow": peer}, device_id_type=MESH)
    for step in range(1, groups):
        peer = lax.rem(outer + step, groups) * group + inner
        pl.semaphore_signal(barrier, inc=1, device_id={"flow": peer}, device_id_type=MESH)

    @pl.when(not_low)
    def _():
        pl.semaphore_signal(barrier, inc=1, device_id={"lat": lat - 1}, device_id_type=MESH)

    @pl.when(not_high)
    def _():
        pl.semaphore_signal(barrier, inc=1, device_id={"lat": lat + 1}, device_id_type=MESH)

    for load in sum(tile_loads, []) + loads:
        load.start()

    nothing = jnp.zeros((3, cells, EDGE, width), jnp.float32)

    @pl.when(lat == 0)
    def _():
        pad[:, :, 0:EDGE] = nothing

    @pl.when(lat == lats - 1)
    def _():
        pad[:, :, EDGE + rows:2 * EDGE + rows] = nothing

    beside = jnp.where(not_low, 1, 0) + jnp.where(not_high, 1, 0)
    pl.semaphore_wait(barrier, group - 1 + groups - 1 + beside)

    to_high = pltpu.make_async_remote_copy(
        src_ref=conc.at[:, :, rows - 1:rows], dst_ref=pad.at[:, :, EDGE - 1:EDGE],
        send_sem=halo_send.at[0], recv_sem=halo_recv.at[0],
        device_id={"lat": lat + 1}, device_id_type=MESH,
    )
    to_low = pltpu.make_async_remote_copy(
        src_ref=conc.at[:, :, 0:1], dst_ref=pad.at[:, :, EDGE + rows:EDGE + rows + 1],
        send_sem=halo_send.at[1], recv_sem=halo_recv.at[1],
        device_id={"lat": lat - 1}, device_id_type=MESH,
    )

    @pl.when(not_high)
    def _():
        to_high.start()

    @pl.when(not_low)
    def _():
        to_low.start()

    matrix, offset = slice(0, 6), slice(6, 9)

    def between(src, dst, there, send, recv, slot, cut, peer, arriving):
        lands = peer if arriving else slot
        return pltpu.make_async_remote_copy(
            src_ref=src.at[peer, cut], dst_ref=dst.at[lands, cut],
            send_sem=send.at[peer], recv_sem=recv.at[lands],
            device_id={"flow": there(peer)}, device_id_type=MESH,
        )

    def member(peer):
        return outer * group + peer

    def matrix_copy(peer, arriving=False):
        return between(mine, maps, member, a_send, a_recv, inner, matrix, peer, arriving)

    def offset_copy(peer, arriving=False):
        return between(mine, maps, member, o_send, o_recv, inner, offset, peer, arriving)

    def flux_copy(peer, arriving=False):
        return between(fluxes, entering, member, c_send, c_recv, inner, slice(0, 3), peer, arriving)

    def put(t, last, values, first, copy):
        for j in range(owners):
            peer = t * owners + j
            for q, value in enumerate(values):
                mine[peer, first + q] = value[j * part:(j + 1) * part]
            if last:
                @pl.when(peer != inner)
                def _():
                    copy(peer).start()
            else:
                copy(peer).start()

    one = jnp.ones((tile, width), jnp.float32)
    zero = jnp.zeros((tile, width), jnp.float32)

    for n, t in enumerate(order):
        for load in tile_loads[n]:
            load.wait()
        at = rows_of(t)

        def matrix_cell(i, state, at=at):
            m00, m10, m11, m20, m21, m22 = state
            c0, c1, c2 = cour[0, i, at], cour[1, i, at], cour[2, i, at]
            k0, k1 = rate[0, i, at], rate[1, i, at]
            r0, r1, r2 = inverse(1.0 + c0 + k0), inverse(1.0 + c1 + k1), inverse(1.0 + c2)
            for k, r in enumerate((r0, r1, r2)):
                inv[k, i, at] = r
            u00 = m00 * r0
            u10 = (m10 + k0 * u00) * r1
            u20 = (m20 + k1 * u10) * r2
            u11 = m11 * r1
            u21 = (m21 + k1 * u11) * r2
            u22 = m22 * r2
            for q, value in enumerate((u00, u10, u11, u20, u21, u22)):
                local[q, i, at] = value
            return c0 * u00, c1 * u10, c1 * u11, c2 * u20, c2 * u21, c2 * u22

        state = lax.fori_loop(
            0, cells, matrix_cell, (one, zero, one, zero, zero, one), unroll=UNROLL
        )
        put(t, n == tiles - 1, state, 0, matrix_copy)

    for load in loads:
        load.wait()

    @pl.when(not_low)
    def _():
        to_high.wait_recv()

    @pl.when(not_high)
    def _():
        to_low.wait_recv()

    lane = lax.broadcasted_iota(jnp.int32, (tile, width), 1)
    first, last = lane == 0, lane == width - 1

    for n, t in enumerate(order):
        at = rows_of(t)
        scale = spr[at]

        def source(k, i, t=t, scale=scale):
            mid = pad[k, i, pl.ds(pl.multiple_of(t * tile + EDGE, EDGE), tile)]
            left = jnp.where(first, 0.0, pltpu.roll(mid, 1, 1))
            right = jnp.where(last, 0.0, pltpu.roll(mid, width - 1, 1))
            up = pad[k, i, pl.ds(t * tile + EDGE - 1, tile)]
            down = pad[k, i, pl.ds(t * tile + EDGE + 1, tile)]
            return mid + scale * (up + down + left + right - 4.0 * mid)

        def offset_cell(i, state, at=at, source=source):
            w0, w1, w2 = state
            v0 = (source(0, i) + w0) * inv[0, i, at]
            v1 = (source(1, i) + w1 + rate[0, i, at] * v0) * inv[1, i, at]
            v2 = (source(2, i) + w2 + rate[1, i, at] * v1) * inv[2, i, at]
            for k, value in enumerate((v0, v1, v2)):
                local[6 + k, i, at] = value
            return cour[0, i, at] * v0, cour[1, i, at] * v1, cour[2, i, at] * v2

        state = lax.fori_loop(0, cells, offset_cell, (zero, zero, zero), unroll=UNROLL)
        put(t, n == tiles - 1, state, 6, offset_copy)

    maps[inner] = mine[inner]

    def map_of(ref, m):
        return tuple(ref[m, q] for q in range(9))

    def group_copy(o, cut, send, recv, arriving):
        lands = o if arriving else outer
        return pltpu.make_async_remote_copy(
            src_ref=total.at[cut], dst_ref=totals.at[lands, cut],
            send_sem=send.at[o], recv_sem=recv.at[lands],
            device_id={"flow": o * group + inner}, device_id_type=MESH,
        )

    def total_matrix(o, arriving=False):
        return group_copy(o, matrix, b_send, b_recv, arriving)

    def total_offset(o, arriving=False):
        return group_copy(o, offset, p_send, p_recv, arriving)

    def to_later(copy):
        for o in reversed(range(1, groups)):
            @pl.when(outer < o)
            def _():
                copy(o).start()

    peers = [lax.rem(inner + step, group) for step in range(1, group)]
    for peer in peers:
        matrix_copy(peer, True).wait_recv()
    if groups > 1:
        product = tuple(maps[0, q] for q in range(6))
        for m in range(1, group):
            product = times(tuple(maps[m, q] for q in range(6)), product)
        for q in range(6):
            total[q] = product[q]
        to_later(total_matrix)
    for peer in peers:
        offset_copy(peer, True).wait_recv()

    flux = tuple(inl[k, pl.ds(pl.multiple_of(inner * part, part), part)] for k in range(3))
    if groups > 1:
        shift = tuple(maps[0, q] for q in range(6, 9))
        for m in range(1, group):
            shift = apply_map(map_of(maps, m), shift)
        for k in range(3):
            total[6 + k] = shift[k]
        to_later(total_offset)

        def earlier(o, flux):
            total_matrix(o, True).wait_recv()
            total_offset(o, True).wait_recv()
            return apply_map(map_of(totals, o), flux)

        flux = lax.fori_loop(0, outer, earlier, flux)

    for m in range(group):
        for k in range(3):
            fluxes[m, k] = flux[k]
        if m < group - 1:
            flux = apply_map(map_of(maps, m), flux)
    for peer in peers:
        flux_copy(peer).start()
    entering[inner] = fluxes[inner]

    for step in range(tiles):
        t = tile_at(step)
        at = rows_of(t)
        for j in range(owners):
            peer = t * owners + j
            if step:
                flux_copy(peer, True).wait_recv()
            else:
                @pl.when(peer != inner)
                def _():
                    flux_copy(peer, True).wait_recv()
        q = [
            jnp.concatenate([entering[t * owners + j, k] for j in range(owners)], axis=0)
            for k in range(3)
        ]

        def finish(i, carry, at=at, q=q):
            fresh = apply_map(tuple(local[n, i, at] for n in range(9)), q)
            for k in range(3):
                out[k, i, at] = fresh[k]
            return carry

        lax.fori_loop(0, cells, finish, 0, unroll=UNROLL)

    for peer in peers:
        matrix_copy(peer).wait_send()
        offset_copy(peer).wait_send()
        flux_copy(peer).wait_send()
    for o in range(1, groups):
        @pl.when(outer < o)
        def _():
            total_matrix(o).wait_send()
            total_offset(o).wait_send()

    @pl.when(not_high)
    def _():
        to_high.wait_send()

    @pl.when(not_low)
    def _():
        to_low.wait_send()


def per_device(flows, lats, concentration, courant, rates, spread, inlet):
    _, cells, rows, width = concentration.shape
    group = GROUP
    groups = flows // group
    part = rows // group
    f32 = jnp.float32
    dma = pltpu.SemaphoreType.DMA
    return pl.pallas_call(
        functools.partial(kernel, groups, group, lats),
        out_shape=jax.ShapeDtypeStruct(concentration.shape, f32),
        in_specs=[pl.BlockSpec(memory_space=pltpu.HBM)] * 5,
        out_specs=pl.BlockSpec(memory_space=pltpu.VMEM),
        scratch_shapes=[
            pltpu.VMEM((3, cells, rows + 2 * EDGE, width), f32),
            pltpu.VMEM((3, cells, rows, width), f32),
            pltpu.VMEM((2, cells, rows, width), f32),
            pltpu.VMEM((rows, width), f32),
            pltpu.VMEM((3, rows, width), f32),
            pltpu.VMEM((9, cells, rows, width), f32),
            pltpu.VMEM((3, cells, rows, width), f32),
            pltpu.VMEM((group, 9, part, width), f32),
            pltpu.VMEM((group, 9, part, width), f32),
            pltpu.VMEM((9, part, width), f32),
            pltpu.VMEM((groups, 9, part, width), f32),
            pltpu.VMEM((group, 3, part, width), f32),
            pltpu.VMEM((group, 3, part, width), f32),
            dma((3,)), dma((2, rows // max(part, EDGE))), dma((2,)), dma((2,)),
            dma((group,)), dma((group,)), dma((group,)), dma((group,)),
            dma((groups,)), dma((groups,)), dma((groups,)), dma((groups,)),
            dma((group,)), dma((group,)),
        ],
        compiler_params=pltpu.CompilerParams(
            collective_id=0, has_side_effects=True, vmem_limit_bytes=24 * 2**20
        ),
        cost_estimate=pl.CostEstimate(
            flops=100 * cells * rows * width, bytes_accessed=44 * cells * rows * width,
            transcendentals=0,
        ),
    )(*(
        pltpu.with_memory_space_constraint(array, pltpu.HBM)
        for array in (concentration, courant, rates, spread, inlet)
    ))


def solution(mesh):
    in_specs = (
        P(None, "flow", "lat", None),
        P(None, "flow", "lat", None),
        P(None, "flow", "lat", None),
        P("lat", None),
        P(None, "lat", None),
    )
    out_specs = P(None, "flow", "lat", None)
    body = functools.partial(per_device, mesh.shape["flow"], mesh.shape["lat"])
    return jax.shard_map(
        body, mesh=mesh, in_specs=in_specs, out_specs=out_specs, check_vma=False
    )
```

```python
import functools
import jax
import jax.numpy as jnp
from jax import lax
from jax.experimental import pallas as pl
from jax.experimental.pallas import tpu as pltpu
from jax.sharding import PartitionSpec as P

MESH = pl.DeviceIdType.MESH
GROUP = 16
EDGE = 8
UNROLL = 16


def apply_map(m, q):
    return (
        m[0] * q[0] + m[6],
        m[1] * q[0] + m[2] * q[1] + m[7],
        m[3] * q[0] + m[4] * q[1] + m[5] * q[2] + m[8],
    )


def times(m, n):
    return (
        m[0] * n[0],
        m[1] * n[0] + m[2] * n[1],
        m[2] * n[2],
        m[3] * n[0] + m[4] * n[1] + m[5] * n[3],
        m[4] * n[2] + m[5] * n[4],
        m[5] * n[5],
    )


def inverse(x):
    rough = pl.reciprocal(x, approx=True)
    return rough * (2.0 - x * rough)


def kernel(
    groups, group, lats,
    conc, courant, rates, spread, inlet, out,
    pad, cour, rate, spr, inl, local, inv, mine, maps, total, totals, fluxes, entering,
    load_sem, tile_sem, halo_send, halo_recv,
    a_send, a_recv, o_send, o_recv, b_send, b_recv, p_send, p_recv, c_send, c_recv,
):
    cells, rows, width = cour.shape[1:]
    part = rows // group
    tile = max(part, EDGE)
    owners = tile // part
    tiles = rows // tile
    flow = lax.axis_index("flow")
    lat = lax.axis_index("lat")
    inner = lax.rem(flow, group)
    outer = lax.div(flow, group)
    not_low, not_high = lat > 0, lat < lats - 1

    def tile_at(step):
        return lax.rem(lax.div(inner, owners) + step, tiles)

    def rows_of(t):
        return pl.ds(pl.multiple_of(t * tile, tile), tile)

    order = [tile_at(step) for step in range(1, tiles)] + [tile_at(0)]
    tile_loads = []
    for n, t in enumerate(order):
        at = rows_of(t)
        tile_loads.append([
            pltpu.make_async_copy(courant.at[:, :, at], cour.at[:, :, at], tile_sem.at[0, n]),
            pltpu.make_async_copy(rates.at[:, :, at], rate.at[:, :, at], tile_sem.at[1, n]),
        ])
    loads = [
        pltpu.make_async_copy(src, dst, load_sem.at[i])
        for i, (src, dst) in enumerate((
            (conc, pad.at[:, :, EDGE:EDGE + rows]), (spread, spr), (inlet, inl),
        ))
    ]
    barrier = pltpu.get_barrier_semaphore()
    for step in range(1, group):
        peer = outer * group + lax.rem(inner + step, group)
        pl.semaphore_signal(barrier, inc=1, device_id={"flow": peer}, device_id_type=MESH)
    for step in range(1, groups):
        peer = lax.rem(outer + step, groups) * group + inner
        pl.semaphore_signal(barrier, inc=1, device_id={"flow": peer}, device_id_type=MESH)

    @pl.when(not_low)
    def _():
        pl.semaphore_signal(barrier, inc=1, device_id={"lat": lat - 1}, device_id_type=MESH)

    @pl.when(not_high)
    def _():
        pl.semaphore_signal(barrier, inc=1, device_id={"lat": lat + 1}, device_id_type=MESH)

    for load in sum(tile_loads, []) + loads:
        load.start()

    nothing = jnp.zeros((3, cells, EDGE, width), jnp.float32)

    @pl.when(lat == 0)
    def _():
        pad[:, :, 0:EDGE] = nothing

    @pl.when(lat == lats - 1)
    def _():
        pad[:, :, EDGE + rows:2 * EDGE + rows] = nothing

    beside = jnp.where(not_low, 1, 0) + jnp.where(not_high, 1, 0)
    pl.semaphore_wait(barrier, group - 1 + groups - 1 + beside)

    to_high = pltpu.make_async_remote_copy(
        src_ref=conc.at[:, :, rows - 1:rows], dst_ref=pad.at[:, :, EDGE - 1:EDGE],
        send_sem=halo_send.at[0], recv_sem=halo_recv.at[0],
        device_id={"lat": lat + 1}, device_id_type=MESH,
    )
    to_low = pltpu.make_async_remote_copy(
        src_ref=conc.at[:, :, 0:1], dst_ref=pad.at[:, :, EDGE + rows:EDGE + rows + 1],
        send_sem=halo_send.at[1], recv_sem=halo_recv.at[1],
        device_id={"lat": lat - 1}, device_id_type=MESH,
    )

    @pl.when(not_high)
    def _():
        to_high.start()

    @pl.when(not_low)
    def _():
        to_low.start()

    matrix, offset = slice(0, 6), slice(6, 9)

    def between(src, dst, there, send, recv, slot, cut, peer, arriving):
        lands = peer if arriving else slot
        return pltpu.make_async_remote_copy(
            src_ref=src.at[peer, cut], dst_ref=dst.at[lands, cut],
            send_sem=send.at[peer], recv_sem=recv.at[lands],
            device_id={"flow": there(peer)}, device_id_type=MESH,
        )

    def member(peer):
        return outer * group + peer

    def matrix_copy(peer, arriving=False):
        return between(mine, maps, member, a_send, a_recv, inner, matrix, peer, arriving)

    def offset_copy(peer, arriving=False):
        return between(mine, maps, member, o_send, o_recv, inner, offset, peer, arriving)

    def flux_copy(peer, arriving=False):
        return between(fluxes, entering, member, c_send, c_recv, inner, slice(0, 3), peer, arriving)

    def put(t, last, values, first, copy):
        for j in range(owners):
            peer = t * owners + j
            for q, value in enumerate(values):
                mine[peer, first + q] = value[j * part:(j + 1) * part]
            if last:
                @pl.when(peer != inner)
                def _():
                    copy(peer).start()
            else:
                copy(peer).start()

    one = jnp.ones((tile, width), jnp.float32)
    zero = jnp.zeros((tile, width), jnp.float32)

    for n, t in enumerate(order):
        for load in tile_loads[n]:
            load.wait()
        at = rows_of(t)

        def matrix_cell(i, state, at=at):
            m00, m10, m11, m20, m21, m22 = state
            c0, c1, c2 = cour[0, i, at], cour[1, i, at], cour[2, i, at]
            k0, k1 = rate[0, i, at], rate[1, i, at]
            r0, r1, r2 = inverse(1.0 + c0 + k0), inverse(1.0 + c1 + k1), inverse(1.0 + c2)
            for k, r in enumerate((r0, r1, r2)):
                inv[k, i, at] = r
            u00 = m00 * r0
            u10 = (m10 + k0 * u00) * r1
            u20 = (m20 + k1 * u10) * r2
            u11 = m11 * r1
            u21 = (m21 + k1 * u11) * r2
            u22 = m22 * r2
            for q, value in enumerate((u00, u10, u11, u20, u21, u22)):
                local[q, i, at] = value
            return c0 * u00, c1 * u10, c1 * u11, c2 * u20, c2 * u21, c2 * u22

        state = lax.fori_loop(
            0, cells, matrix_cell, (one, zero, one, zero, zero, one), unroll=UNROLL
        )
        put(t, n == tiles - 1, state, 0, matrix_copy)

    for load in loads:
        load.wait()

    @pl.when(not_low)
    def _():
        to_high.wait_recv()

    @pl.when(not_high)
    def _():
        to_low.wait_recv()

    lane = lax.broadcasted_iota(jnp.int32, (tile, width), 1)
    first, last = lane == 0, lane == width - 1

    for n, t in enumerate(order):
        at = rows_of(t)
        scale = spr[at]

        def source(k, i, t=t, scale=scale):
            mid = pad[k, i, pl.ds(pl.multiple_of(t * tile + EDGE, EDGE), tile)]
            left = jnp.where(first, 0.0, pltpu.roll(mid, 1, 1))
            right = jnp.where(last, 0.0, pltpu.roll(mid, width - 1, 1))
            up = pad[k, i, pl.ds(t * tile + EDGE - 1, tile)]
            down = pad[k, i, pl.ds(t * tile + EDGE + 1, tile)]
            return mid + scale * (up + down + left + right - 4.0 * mid)

        def offset_cell(i, state, at=at, source=source):
            w0, w1, w2 = state
            v0 = (source(0, i) + w0) * inv[0, i, at]
            v1 = (source(1, i) + w1 + rate[0, i, at] * v0) * inv[1, i, at]
            v2 = (source(2, i) + w2 + rate[1, i, at] * v1) * inv[2, i, at]
            for k, value in enumerate((v0, v1, v2)):
                local[6 + k, i, at] = value
            return cour[0, i, at] * v0, cour[1, i, at] * v1, cour[2, i, at] * v2

        state = lax.fori_loop(0, cells, offset_cell, (zero, zero, zero), unroll=UNROLL)
        put(t, n == tiles - 1, state, 6, offset_copy)

    maps[inner] = mine[inner]

    def map_of(ref, m):
        return tuple(ref[m, q] for q in range(9))

    def group_copy(o, cut, send, recv, arriving):
        lands = o if arriving else outer
        return pltpu.make_async_remote_copy(
            src_ref=total.at[cut], dst_ref=totals.at[lands, cut],
            send_sem=send.at[o], recv_sem=recv.at[lands],
            device_id={"flow": o * group + inner}, device_id_type=MESH,
        )

    def total_matrix(o, arriving=False):
        return group_copy(o, matrix, b_send, b_recv, arriving)

    def total_offset(o, arriving=False):
        return group_copy(o, offset, p_send, p_recv, arriving)

    def to_later(copy):
        for o in reversed(range(1, groups)):
            @pl.when(outer < o)
            def _():
                copy(o).start()

    peers = [lax.rem(inner + step, group) for step in range(1, group)]
    for peer in peers:
        matrix_copy(peer, True).wait_recv()
    if groups > 1:
        product = tuple(maps[0, q] for q in range(6))
        for m in range(1, group):
            product = times(tuple(maps[m, q] for q in range(6)), product)
        for q in range(6):
            total[q] = product[q]
        to_later(total_matrix)
    for peer in peers:
        offset_copy(peer, True).wait_recv()

    flux = tuple(inl[k, pl.ds(pl.multiple_of(inner * part, part), part)] for k in range(3))
    if groups > 1:
        shift = tuple(maps[0, q] for q in range(6, 9))
        for m in range(1, group):
            shift = apply_map(map_of(maps, m), shift)
        for k in range(3):
            total[6 + k] = shift[k]
        to_later(total_offset)

        def earlier(o, flux):
            total_matrix(o, True).wait_recv()
            total_offset(o, True).wait_recv()
            return apply_map(map_of(totals, o), flux)

        flux = lax.fori_loop(0, outer, earlier, flux)

    for m in range(group):
        for k in range(3):
            fluxes[m, k] = flux[k]
        if m < group - 1:
            flux = apply_map(map_of(maps, m), flux)
    for peer in peers:
        flux_copy(peer).start()
    entering[inner] = fluxes[inner]

    for step in range(tiles):
        t = tile_at(step)
        at = rows_of(t)
        for j in range(owners):
            peer = t * owners + j
            if step:
                flux_copy(peer, True).wait_recv()
            else:
                @pl.when(peer != inner)
                def _():
                    flux_copy(peer, True).wait_recv()
        q = [
            jnp.concatenate([entering[t * owners + j, k] for j in range(owners)], axis=0)
            for k in range(3)
        ]

        def finish(i, carry, at=at, q=q):
            fresh = apply_map(tuple(local[n, i, at] for n in range(9)), q)
            for k in range(3):
                out[k, i, at] = fresh[k]
            return carry

        lax.fori_loop(0, cells, finish, 0, unroll=UNROLL)

    for peer in peers:
        matrix_copy(peer).wait_send()
        offset_copy(peer).wait_send()
        flux_copy(peer).wait_send()
    for o in range(1, groups):
        @pl.when(outer < o)
        def _():
            total_matrix(o).wait_send()
            total_offset(o).wait_send()

    @pl.when(not_high)
    def _():
        to_high.wait_send()

    @pl.when(not_low)
    def _():
        to_low.wait_send()


def per_device(flows, lats, concentration, courant, rates, spread, inlet):
    _, cells, rows, width = concentration.shape
    group = GROUP
    groups = flows // group
    part = rows // group
    f32 = jnp.float32
    dma = pltpu.SemaphoreType.DMA
    return pl.pallas_call(
        functools.partial(kernel, groups, group, lats),
        out_shape=jax.ShapeDtypeStruct(concentration.shape, f32),
        in_specs=[pl.BlockSpec(memory_space=pltpu.HBM)] * 5,
        out_specs=pl.BlockSpec(memory_space=pltpu.VMEM),
        scratch_shapes=[
            pltpu.VMEM((3, cells, rows + 2 * EDGE, width), f32),
            pltpu.VMEM((3, cells, rows, width), f32),
            pltpu.VMEM((2, cells, rows, width), f32),
            pltpu.VMEM((rows, width), f32),
            pltpu.VMEM((3, rows, width), f32),
            pltpu.VMEM((9, cells, rows, width), f32),
            pltpu.VMEM((3, cells, rows, width), f32),
            pltpu.VMEM((group, 9, part, width), f32),
            pltpu.VMEM((group, 9, part, width), f32),
            pltpu.VMEM((9, part, width), f32),
            pltpu.VMEM((groups, 9, part, width), f32),
            pltpu.VMEM((group, 3, part, width), f32),
            pltpu.VMEM((group, 3, part, width), f32),
            dma((3,)), dma((2, rows // max(part, EDGE))), dma((2,)), dma((2,)),
            dma((group,)), dma((group,)), dma((group,)), dma((group,)),
            dma((groups,)), dma((groups,)), dma((groups,)), dma((groups,)),
            dma((group,)), dma((group,)),
        ],
        compiler_params=pltpu.CompilerParams(
            collective_id=0, has_side_effects=True, vmem_limit_bytes=24 * 2**20
        ),
        cost_estimate=pl.CostEstimate(
            flops=100 * cells * rows * width, bytes_accessed=44 * cells * rows * width,
            transcendentals=0,
        ),
    )(*(
        pltpu.with_memory_space_constraint(array, pltpu.HBM)
        for array in (concentration, courant, rates, spread, inlet)
    ))


def solution(mesh):
    in_specs = (
        P(None, "flow", "lat", None),
        P(None, "flow", "lat", None),
        P(None, "flow", "lat", None),
        P("lat", None),
        P(None, "lat", None),
    )
    out_specs = P(None, "flow", "lat", None)
    body = functools.partial(per_device, mesh.shape["flow"], mesh.shape["lat"])
    return jax.shard_map(
        body, mesh=mesh, in_specs=in_specs, out_specs=out_specs, check_vma=False
    )
```

```python
import functools
import jax
import jax.numpy as jnp
from jax import lax
from jax.experimental import pallas as pl
from jax.experimental.pallas import tpu as pltpu
from jax.sharding import PartitionSpec as P

MESH = pl.DeviceIdType.MESH
GROUP = 4
EDGE = 8
UNROLL = 16


def apply_map(m, q):
    return (
        m[0] * q[0] + m[6],
        m[1] * q[0] + m[2] * q[1] + m[7],
        m[3] * q[0] + m[4] * q[1] + m[5] * q[2] + m[8],
    )


def times(m, n):
    return (
        m[0] * n[0],
        m[1] * n[0] + m[2] * n[1],
        m[2] * n[2],
        m[3] * n[0] + m[4] * n[1] + m[5] * n[3],
        m[4] * n[2] + m[5] * n[4],
        m[5] * n[5],
    )


def inverse(x):
    rough = pl.reciprocal(x, approx=True)
    return rough * (2.0 - x * rough)


def kernel(
    groups, group, lats,
    conc, courant, rates, spread, inlet, out,
    pad, cour, rate, spr, inl, local, inv, mine, maps, total, totals, fluxes, entering,
    load_sem, tile_sem, halo_send, halo_recv,
    a_send, a_recv, o_send, o_recv, b_send, b_recv, p_send, p_recv, c_send, c_recv,
):
    cells, rows, width = cour.shape[1:]
    part = rows // group
    tile = max(part, EDGE)
    owners = tile // part
    tiles = rows // tile
    flow = lax.axis_index("flow")
    lat = lax.axis_index("lat")
    inner = lax.rem(flow, group)
    outer = lax.div(flow, group)
    not_low, not_high = lat > 0, lat < lats - 1

    def tile_at(step):
        return lax.rem(lax.div(inner, owners) + step, tiles)

    def rows_of(t):
        return pl.ds(pl.multiple_of(t * tile, tile), tile)

    def nth(n):
        return tile_at(n + 1)

    def tile_loads(n):
        at = rows_of(nth(n))
        return (
            pltpu.make_async_copy(courant.at[:, :, at], cour.at[:, :, at], tile_sem.at[0, n]),
            pltpu.make_async_copy(rates.at[:, :, at], rate.at[:, :, at], tile_sem.at[1, n]),
        )

    loads = [
        pltpu.make_async_copy(src, dst, load_sem.at[i])
        for i, (src, dst) in enumerate((
            (conc, pad.at[:, :, EDGE:EDGE + rows]), (spread, spr), (inlet, inl),
        ))
    ]
    barrier = pltpu.get_barrier_semaphore()
    for step in range(1, group):
        peer = outer * group + lax.rem(inner + step, group)
        pl.semaphore_signal(barrier, inc=1, device_id={"flow": peer}, device_id_type=MESH)
    for step in range(1, groups):
        peer = lax.rem(outer + step, groups) * group + inner
        pl.semaphore_signal(barrier, inc=1, device_id={"flow": peer}, device_id_type=MESH)

    @pl.when(not_low)
    def _():
        pl.semaphore_signal(barrier, inc=1, device_id={"lat": lat - 1}, device_id_type=MESH)

    @pl.when(not_high)
    def _():
        pl.semaphore_signal(barrier, inc=1, device_id={"lat": lat + 1}, device_id_type=MESH)

    for n in range(tiles):
        for load in tile_loads(n):
            load.start()
    for load in loads:
        load.start()

    nothing = jnp.zeros((3, cells, EDGE, width), jnp.float32)

    @pl.when(lat == 0)
    def _():
        pad[:, :, 0:EDGE] = nothing

    @pl.when(lat == lats - 1)
    def _():
        pad[:, :, EDGE + rows:2 * EDGE + rows] = nothing

    beside = jnp.where(not_low, 1, 0) + jnp.where(not_high, 1, 0)
    pl.semaphore_wait(barrier, group - 1 + groups - 1 + beside)

    to_high = pltpu.make_async_remote_copy(
        src_ref=conc.at[:, :, rows - 1:rows], dst_ref=pad.at[:, :, EDGE - 1:EDGE],
        send_sem=halo_send.at[0], recv_sem=halo_recv.at[0],
        device_id={"lat": lat + 1}, device_id_type=MESH,
    )
    to_low = pltpu.make_async_remote_copy(
        src_ref=conc.at[:, :, 0:1], dst_ref=pad.at[:, :, EDGE + rows:EDGE + rows + 1],
        send_sem=halo_send.at[1], recv_sem=halo_recv.at[1],
        device_id={"lat": lat - 1}, device_id_type=MESH,
    )

    @pl.when(not_high)
    def _():
        to_high.start()

    @pl.when(not_low)
    def _():
        to_low.start()

    matrix, offset = slice(0, 6), slice(6, 9)

    def between(src, dst, there, send, recv, slot, cut, peer, arriving):
        lands = peer if arriving else slot
        return pltpu.make_async_remote_copy(
            src_ref=src.at[peer, cut], dst_ref=dst.at[lands, cut],
            send_sem=send.at[peer], recv_sem=recv.at[lands],
            device_id={"flow": there(peer)}, device_id_type=MESH,
        )

    def member(peer):
        return outer * group + peer

    def matrix_copy(peer, arriving=False):
        return between(mine, maps, member, a_send, a_recv, inner, matrix, peer, arriving)

    def offset_copy(peer, arriving=False):
        return between(mine, maps, member, o_send, o_recv, inner, offset, peer, arriving)

    def flux_copy(peer, arriving=False):
        return between(fluxes, entering, member, c_send, c_recv, inner, slice(0, 3), peer, arriving)

    def put(t, values, first, copy):
        for j in range(owners):
            peer = t * owners + j
            for q, value in enumerate(values):
                mine[peer, first + q] = value[j * part:(j + 1) * part]

            @pl.when(peer != inner)
            def _():
                copy(peer).start()

    one = jnp.ones((tile, width), jnp.float32)
    zero = jnp.zeros((tile, width), jnp.float32)

    def matrix_tile(n, carry):
        for load in tile_loads(n):
            load.wait()
        t = nth(n)
        at = rows_of(t)

        def matrix_cell(i, state):
            m00, m10, m11, m20, m21, m22 = state
            c0, c1, c2 = cour[0, i, at], cour[1, i, at], cour[2, i, at]
            k0, k1 = rate[0, i, at], rate[1, i, at]
            r0, r1, r2 = inverse(1.0 + c0 + k0), inverse(1.0 + c1 + k1), inverse(1.0 + c2)
            for k, r in enumerate((r0, r1, r2)):
                inv[k, i, at] = r
            u00 = m00 * r0
            u10 = (m10 + k0 * u00) * r1
            u20 = (m20 + k1 * u10) * r2
            u11 = m11 * r1
            u21 = (m21 + k1 * u11) * r2
            u22 = m22 * r2
            for q, value in enumerate((u00, u10, u11, u20, u21, u22)):
                local[q, i, at] = value
            return c0 * u00, c1 * u10, c1 * u11, c2 * u20, c2 * u21, c2 * u22

        state = lax.fori_loop(
            0, cells, matrix_cell, (one, zero, one, zero, zero, one), unroll=UNROLL
        )
        put(t, state, 0, matrix_copy)
        return carry

    lax.fori_loop(0, tiles, matrix_tile, 0)

    for load in loads:
        load.wait()

    @pl.when(not_low)
    def _():
        to_high.wait_recv()

    @pl.when(not_high)
    def _():
        to_low.wait_recv()

    lane = lax.broadcasted_iota(jnp.int32, (tile, width), 1)
    first, last = lane == 0, lane == width - 1

    def group_copy(o, cut, send, recv, arriving):
        lands = o if arriving else outer
        return pltpu.make_async_remote_copy(
            src_ref=total.at[cut], dst_ref=totals.at[lands, cut],
            send_sem=send.at[o], recv_sem=recv.at[lands],
            device_id={"flow": o * group + inner}, device_id_type=MESH,
        )

    def total_matrix(o, arriving=False):
        return group_copy(o, matrix, b_send, b_recv, arriving)

    def total_offset(o, arriving=False):
        return group_copy(o, offset, p_send, p_recv, arriving)

    peers = [lax.rem(inner + step, group) for step in range(1, group)]

    def fold_matrices():
        maps[inner, matrix] = mine[inner, matrix]
        for peer in peers:
            matrix_copy(peer, True).wait_recv()

        if groups > 2:
            @pl.when((outer > 0) & (outer < groups - 1))
            def _():
                product = tuple(maps[0, q] for q in range(6))
                for m in range(1, group):
                    product = times(tuple(maps[m, q] for q in range(6)), product)
                for q in range(6):
                    total[q] = product[q]
                for o in reversed(range(2, groups)):
                    @pl.when(outer < o)
                    def _():
                        total_matrix(o).start()

    def offset_tile(n, carry):
        @pl.when(n == tiles - 1)
        def _():
            fold_matrices()

        t = nth(n)
        at = rows_of(t)
        scale = spr[at]

        def source(k, i):
            mid = pad[k, i, pl.ds(pl.multiple_of(t * tile + EDGE, EDGE), tile)]
            left = jnp.where(first, 0.0, pltpu.roll(mid, 1, 1))
            right = jnp.where(last, 0.0, pltpu.roll(mid, width - 1, 1))
            up = pad[k, i, pl.ds(t * tile + EDGE - 1, tile)]
            down = pad[k, i, pl.ds(t * tile + EDGE + 1, tile)]
            return mid + scale * (up + down + left + right - 4.0 * mid)

        def offset_cell(i, state):
            w0, w1, w2 = state
            v0 = (source(0, i) + w0) * inv[0, i, at]
            v1 = (source(1, i) + w1 + rate[0, i, at] * v0) * inv[1, i, at]
            v2 = (source(2, i) + w2 + rate[1, i, at] * v1) * inv[2, i, at]
            for k, value in enumerate((v0, v1, v2)):
                local[6 + k, i, at] = value
            return cour[0, i, at] * v0, cour[1, i, at] * v1, cour[2, i, at] * v2

        state = lax.fori_loop(0, cells, offset_cell, (zero, zero, zero), unroll=UNROLL)
        put(t, state, 6, offset_copy)
        return carry

    lax.fori_loop(0, tiles, offset_tile, 0)

    def map_of(ref, m):
        return tuple(ref[m, q] for q in range(9))

    maps[inner, offset] = mine[inner, offset]
    for peer in peers:
        offset_copy(peer, True).wait_recv()

    inflow = tuple(inl[k, pl.ds(pl.multiple_of(inner * part, part), part)] for k in range(3))
    if groups > 1:
        shift = tuple(jnp.where(outer == 0, value, 0.0) for value in inflow)
        for m in range(group):
            shift = apply_map(map_of(maps, m), shift)
        for k in range(3):
            total[6 + k] = shift[k]
        for o in reversed(range(1, groups)):
            @pl.when(outer < o)
            def _():
                total_offset(o).start()

        @pl.when(outer > 0)
        def _():
            total_offset(0, True).wait_recv()

        def earlier(o, flux):
            total_matrix(o, True).wait_recv()
            total_offset(o, True).wait_recv()
            return apply_map(map_of(totals, o), flux)

        @pl.when(outer == 0)
        def _():
            for k in range(3):
                fluxes[0, k] = inflow[k]

        @pl.when(outer > 0)
        def _():
            flux = lax.fori_loop(1, outer, earlier, tuple(totals[0, 6 + k] for k in range(3)))
            for k in range(3):
                fluxes[0, k] = flux[k]
    else:
        for k in range(3):
            fluxes[0, k] = inflow[k]

    flux = tuple(fluxes[0, k] for k in range(3))
    for m in range(1, group):
        flux = apply_map(map_of(maps, m - 1), flux)
        for k in range(3):
            fluxes[m, k] = flux[k]
    for peer in peers:
        flux_copy(peer).start()
    entering[inner] = fluxes[inner]

    def finish_tile(step, carry):
        t = tile_at(step)
        at = rows_of(t)
        for j in range(owners):
            peer = t * owners + j

            @pl.when(peer != inner)
            def _():
                flux_copy(peer, True).wait_recv()
        q = [
            jnp.concatenate([entering[t * owners + j, k] for j in range(owners)], axis=0)
            for k in range(3)
        ]

        def finish(i, carry):
            fresh = apply_map(tuple(local[n, i, at] for n in range(9)), q)
            for k in range(3):
                out[k, i, at] = fresh[k]
            return carry

        return lax.fori_loop(0, cells, finish, carry, unroll=UNROLL)

    lax.fori_loop(0, tiles, finish_tile, 0)

    for peer in peers:
        matrix_copy(peer).wait_send()
        offset_copy(peer).wait_send()
        flux_copy(peer).wait_send()
    for o in range(1, groups):
        @pl.when(outer < o)
        def _():
            total_offset(o).wait_send()

        @pl.when((outer > 0) & (outer < o))
        def _():
            total_matrix(o).wait_send()

    @pl.when(not_high)
    def _():
        to_high.wait_send()

    @pl.when(not_low)
    def _():
        to_low.wait_send()


def per_device(flows, lats, concentration, courant, rates, spread, inlet):
    _, cells, rows, width = concentration.shape
    group = GROUP
    groups = flows // group
    part = rows // group
    f32 = jnp.float32
    dma = pltpu.SemaphoreType.DMA
    return pl.pallas_call(
        functools.partial(kernel, groups, group, lats),
        out_shape=jax.ShapeDtypeStruct(concentration.shape, f32),
        in_specs=[pl.BlockSpec(memory_space=pltpu.HBM)] * 5,
        out_specs=pl.BlockSpec(memory_space=pltpu.VMEM),
        scratch_shapes=[
            pltpu.VMEM((3, cells, rows + 2 * EDGE, width), f32),
            pltpu.VMEM((3, cells, rows, width), f32),
            pltpu.VMEM((2, cells, rows, width), f32),
            pltpu.VMEM((rows, width), f32),
            pltpu.VMEM((3, rows, width), f32),
            pltpu.VMEM((9, cells, rows, width), f32),
            pltpu.VMEM((3, cells, rows, width), f32),
            pltpu.VMEM((group, 9, part, width), f32),
            pltpu.VMEM((group, 9, part, width), f32),
            pltpu.VMEM((9, part, width), f32),
            pltpu.VMEM((groups, 9, part, width), f32),
            pltpu.VMEM((group, 3, part, width), f32),
            pltpu.VMEM((group, 3, part, width), f32),
            dma((3,)), dma((2, rows // max(part, EDGE))), dma((2,)), dma((2,)),
            dma((group,)), dma((group,)), dma((group,)), dma((group,)),
            dma((groups,)), dma((groups,)), dma((groups,)), dma((groups,)),
            dma((group,)), dma((group,)),
        ],
        compiler_params=pltpu.CompilerParams(
            collective_id=0, has_side_effects=True, vmem_limit_bytes=24 * 2**20
        ),
        cost_estimate=pl.CostEstimate(
            flops=100 * cells * rows * width, bytes_accessed=44 * cells * rows * width,
            transcendentals=0,
        ),
    )(*(
        pltpu.with_memory_space_constraint(array, pltpu.HBM)
        for array in (concentration, courant, rates, spread, inlet)
    ))


def solution(mesh):
    in_specs = (
        P(None, "flow", "lat", None),
        P(None, "flow", "lat", None),
        P(None, "flow", "lat", None),
        P("lat", None),
        P(None, "lat", None),
    )
    out_specs = P(None, "flow", "lat", None)
    body = functools.partial(per_device, mesh.shape["flow"], mesh.shape["lat"])
    return jax.shard_map(
        body, mesh=mesh, in_specs=in_specs, out_specs=out_specs, check_vma=False
    )
```

```python
import functools
import jax
import jax.numpy as jnp
from jax import lax
from jax.experimental import pallas as pl
from jax.experimental.pallas import tpu as pltpu
from jax.sharding import PartitionSpec as P

MESH = pl.DeviceIdType.MESH
GROUP = 4
EDGE = 8
UNROLL = 16


def apply_map(m, q):
    return (
        m[0] * q[0] + m[6],
        m[1] * q[0] + m[2] * q[1] + m[7],
        m[3] * q[0] + m[4] * q[1] + m[5] * q[2] + m[8],
    )


def times(m, n):
    return (
        m[0] * n[0],
        m[1] * n[0] + m[2] * n[1],
        m[2] * n[2],
        m[3] * n[0] + m[4] * n[1] + m[5] * n[3],
        m[4] * n[2] + m[5] * n[4],
        m[5] * n[5],
    )


def inverse(x):
    rough = pl.reciprocal(x, approx=True)
    return rough * (2.0 - x * rough)


def kernel(
    groups, group, lats,
    conc, courant, rates, spread, inlet, out,
    pad, cour, rate, spr, inl, local, inv, mine, maps, total, totals, fluxes, entering,
    load_sem, tile_sem, halo_send, halo_recv,
    a_send, a_recv, o_send, o_recv, b_send, b_recv, p_send, p_recv, c_send, c_recv,
):
    cells, rows, width = cour.shape[1:]
    part = rows // group
    tile = max(part, EDGE)
    owners = tile // part
    tiles = rows // tile
    flow = lax.axis_index("flow")
    lat = lax.axis_index("lat")
    inner = lax.rem(flow, group)
    outer = lax.div(flow, group)
    not_low, not_high = lat > 0, lat < lats - 1

    def tile_at(step):
        return lax.rem(lax.div(inner, owners) + step, tiles)

    def rows_of(t):
        return pl.ds(pl.multiple_of(t * tile, tile), tile)

    def nth(n):
        return tile_at(n + 1)

    def tile_loads(n):
        at = rows_of(nth(n))
        return (
            pltpu.make_async_copy(courant.at[:, :, at], cour.at[:, :, at], tile_sem.at[0, n]),
            pltpu.make_async_copy(rates.at[:, :, at], rate.at[:, :, at], tile_sem.at[1, n]),
        )

    loads = [
        pltpu.make_async_copy(src, dst, load_sem.at[i])
        for i, (src, dst) in enumerate((
            (conc, pad.at[:, :, EDGE:EDGE + rows]), (spread, spr), (inlet, inl),
        ))
    ]
    barrier = pltpu.get_barrier_semaphore()
    for step in range(1, group):
        peer = outer * group + lax.rem(inner + step, group)
        pl.semaphore_signal(barrier, inc=1, device_id={"flow": peer}, device_id_type=MESH)
    for step in range(1, groups):
        peer = lax.rem(outer + step, groups) * group + inner
        pl.semaphore_signal(barrier, inc=1, device_id={"flow": peer}, device_id_type=MESH)

    @pl.when(not_low)
    def _():
        pl.semaphore_signal(barrier, inc=1, device_id={"lat": lat - 1}, device_id_type=MESH)

    @pl.when(not_high)
    def _():
        pl.semaphore_signal(barrier, inc=1, device_id={"lat": lat + 1}, device_id_type=MESH)

    for n in range(tiles):
        for load in tile_loads(n):
            load.start()
    for load in loads:
        load.start()

    nothing = jnp.zeros((3, cells, EDGE, width), jnp.float32)

    @pl.when(lat == 0)
    def _():
        pad[:, :, 0:EDGE] = nothing

    @pl.when(lat == lats - 1)
    def _():
        pad[:, :, EDGE + rows:2 * EDGE + rows] = nothing

    beside = jnp.where(not_low, 1, 0) + jnp.where(not_high, 1, 0)
    pl.semaphore_wait(barrier, group - 1 + groups - 1 + beside)

    to_high = pltpu.make_async_remote_copy(
        src_ref=conc.at[:, :, rows - 1:rows], dst_ref=pad.at[:, :, EDGE - 1:EDGE],
        send_sem=halo_send.at[0], recv_sem=halo_recv.at[0],
        device_id={"lat": lat + 1}, device_id_type=MESH,
    )
    to_low = pltpu.make_async_remote_copy(
        src_ref=conc.at[:, :, 0:1], dst_ref=pad.at[:, :, EDGE + rows:EDGE + rows + 1],
        send_sem=halo_send.at[1], recv_sem=halo_recv.at[1],
        device_id={"lat": lat - 1}, device_id_type=MESH,
    )

    @pl.when(not_high)
    def _():
        to_high.start()

    @pl.when(not_low)
    def _():
        to_low.start()

    matrix, offset = slice(0, 6), slice(6, 9)

    def between(src, dst, there, send, recv, slot, cut, peer, arriving):
        lands = peer if arriving else slot
        return pltpu.make_async_remote_copy(
            src_ref=src.at[peer, cut], dst_ref=dst.at[lands, cut],
            send_sem=send.at[peer], recv_sem=recv.at[lands],
            device_id={"flow": there(peer)}, device_id_type=MESH,
        )

    def member(peer):
        return outer * group + peer

    def matrix_copy(peer, arriving=False):
        return between(mine, maps, member, a_send, a_recv, inner, matrix, peer, arriving)

    def offset_copy(peer, arriving=False):
        return between(mine, maps, member, o_send, o_recv, inner, offset, peer, arriving)

    def flux_copy(peer, arriving=False):
        return between(fluxes, entering, member, c_send, c_recv, inner, slice(0, 3), peer, arriving)

    def put(t, values, first, copy):
        for j in range(owners):
            peer = t * owners + j
            for q, value in enumerate(values):
                mine[peer, first + q] = value[j * part:(j + 1) * part]

            @pl.when(peer != inner)
            def _():
                copy(peer).start()

    one = jnp.ones((tile, width), jnp.float32)
    zero = jnp.zeros((tile, width), jnp.float32)

    def matrix_tile(n, carry):
        for load in tile_loads(n):
            load.wait()
        t = nth(n)
        at = rows_of(t)

        def matrix_cell(i, state):
            m00, m10, m11, m20, m21, m22 = state
            c0, c1, c2 = cour[0, i, at], cour[1, i, at], cour[2, i, at]
            k0, k1 = rate[0, i, at], rate[1, i, at]
            r0, r1, r2 = inverse(1.0 + c0 + k0), inverse(1.0 + c1 + k1), inverse(1.0 + c2)
            for k, r in enumerate((r0, r1, r2)):
                inv[k, i, at] = r
            u00 = m00 * r0
            u10 = (m10 + k0 * u00) * r1
            u20 = (m20 + k1 * u10) * r2
            u11 = m11 * r1
            u21 = (m21 + k1 * u11) * r2
            u22 = m22 * r2
            for q, value in enumerate((u00, u10, u11, u20, u21, u22)):
                local[q, i, at] = value
            return c0 * u00, c1 * u10, c1 * u11, c2 * u20, c2 * u21, c2 * u22

        state = lax.fori_loop(
            0, cells, matrix_cell, (one, zero, one, zero, zero, one), unroll=UNROLL
        )
        put(t, state, 0, matrix_copy)
        return carry

    lax.fori_loop(0, tiles, matrix_tile, 0)

    for load in loads:
        load.wait()

    lane = lax.broadcasted_iota(jnp.int32, (tile, width), 1)
    first, last = lane == 0, lane == width - 1

    def group_copy(o, cut, send, recv, arriving):
        lands = o if arriving else outer
        return pltpu.make_async_remote_copy(
            src_ref=total.at[cut], dst_ref=totals.at[lands, cut],
            send_sem=send.at[o], recv_sem=recv.at[lands],
            device_id={"flow": o * group + inner}, device_id_type=MESH,
        )

    def total_matrix(o, arriving=False):
        return group_copy(o, matrix, b_send, b_recv, arriving)

    def total_offset(o, arriving=False):
        return group_copy(o, offset, p_send, p_recv, arriving)

    peers = [lax.rem(inner + step, group) for step in range(1, group)]

    def fold_matrices():
        maps[inner, matrix] = mine[inner, matrix]
        for peer in peers:
            matrix_copy(peer, True).wait_recv()

        if groups > 2:
            @pl.when((outer > 0) & (outer < groups - 1))
            def _():
                product = tuple(maps[0, q] for q in range(6))
                for m in range(1, group):
                    product = times(tuple(maps[m, q] for q in range(6)), product)
                for q in range(6):
                    total[q] = product[q]
                for o in range(2, groups):
                    @pl.when(outer < o)
                    def _():
                        total_matrix(o).start()

    last_inside = tiles - 1 - jnp.where(not_low & not_high, 1, 0)

    def offset_tile(n, carry):
        @pl.when((n == last_inside) & not_low)
        def _():
            to_high.wait_recv()

        @pl.when((n == last_inside) & not_high)
        def _():
            to_low.wait_recv()

        t = lax.rem(n + jnp.where(not_low, 1, 0), tiles)
        at = rows_of(t)
        scale = spr[at]

        def source(k, i):
            mid = pad[k, i, pl.ds(pl.multiple_of(t * tile + EDGE, EDGE), tile)]
            left = jnp.where(first, 0.0, pltpu.roll(mid, 1, 1))
            right = jnp.where(last, 0.0, pltpu.roll(mid, width - 1, 1))
            up = pad[k, i, pl.ds(t * tile + EDGE - 1, tile)]
            down = pad[k, i, pl.ds(t * tile + EDGE + 1, tile)]
            return mid + scale * (up + down + left + right - 4.0 * mid)

        def offset_cell(i, state):
            w0, w1, w2 = state
            v0 = (source(0, i) + w0) * inv[0, i, at]
            v1 = (source(1, i) + w1 + rate[0, i, at] * v0) * inv[1, i, at]
            v2 = (source(2, i) + w2 + rate[1, i, at] * v1) * inv[2, i, at]
            for k, value in enumerate((v0, v1, v2)):
                local[6 + k, i, at] = value
            return cour[0, i, at] * v0, cour[1, i, at] * v1, cour[2, i, at] * v2

        state = lax.fori_loop(0, cells, offset_cell, (zero, zero, zero), unroll=UNROLL)
        put(t, state, 6, offset_copy)
        return carry

    lax.fori_loop(0, tiles, offset_tile, 0)
    fold_matrices()

    def map_of(ref, m):
        return tuple(ref[m, q] for q in range(9))

    maps[inner, offset] = mine[inner, offset]
    for peer in peers:
        offset_copy(peer, True).wait_recv()

    inflow = tuple(inl[k, pl.ds(pl.multiple_of(inner * part, part), part)] for k in range(3))
    if groups > 1:
        shift = tuple(jnp.where(outer == 0, value, 0.0) for value in inflow)
        for m in range(group):
            shift = apply_map(map_of(maps, m), shift)
        for k in range(3):
            total[6 + k] = shift[k]
        for o in range(1, groups):
            @pl.when(outer < o)
            def _():
                total_offset(o).start()

        @pl.when(outer > 0)
        def _():
            total_offset(0, True).wait_recv()

        def earlier(o, flux):
            total_matrix(o, True).wait_recv()
            total_offset(o, True).wait_recv()
            return apply_map(map_of(totals, o), flux)

        @pl.when(outer == 0)
        def _():
            for k in range(3):
                fluxes[0, k] = inflow[k]

        @pl.when(outer > 0)
        def _():
            flux = lax.fori_loop(1, outer, earlier, tuple(totals[0, 6 + k] for k in range(3)))
            for k in range(3):
                fluxes[0, k] = flux[k]
    else:
        for k in range(3):
            fluxes[0, k] = inflow[k]

    flux = tuple(fluxes[0, k] for k in range(3))
    for m in range(1, group):
        flux = apply_map(map_of(maps, m - 1), flux)
        for k in range(3):
            fluxes[m, k] = flux[k]
    for peer in peers:
        flux_copy(peer).start()
    entering[inner] = fluxes[inner]

    def finish_tile(step, carry):
        t = tile_at(step)
        at = rows_of(t)
        for j in range(owners):
            peer = t * owners + j

            @pl.when(peer != inner)
            def _():
                flux_copy(peer, True).wait_recv()
        q = [
            jnp.concatenate([entering[t * owners + j, k] for j in range(owners)], axis=0)
            for k in range(3)
        ]

        def finish(i, carry):
            fresh = apply_map(tuple(local[n, i, at] for n in range(9)), q)
            for k in range(3):
                out[k, i, at] = fresh[k]
            return carry

        return lax.fori_loop(0, cells, finish, carry, unroll=UNROLL)

    lax.fori_loop(0, tiles, finish_tile, 0)

    for peer in peers:
        matrix_copy(peer).wait_send()
        offset_copy(peer).wait_send()
        flux_copy(peer).wait_send()
    for o in range(1, groups):
        @pl.when(outer < o)
        def _():
            total_offset(o).wait_send()

        @pl.when((outer > 0) & (outer < o))
        def _():
            total_matrix(o).wait_send()

    @pl.when(not_high)
    def _():
        to_high.wait_send()

    @pl.when(not_low)
    def _():
        to_low.wait_send()


def per_device(flows, lats, concentration, courant, rates, spread, inlet):
    _, cells, rows, width = concentration.shape
    group = GROUP
    groups = flows // group
    part = rows // group
    f32 = jnp.float32
    dma = pltpu.SemaphoreType.DMA
    return pl.pallas_call(
        functools.partial(kernel, groups, group, lats),
        out_shape=jax.ShapeDtypeStruct(concentration.shape, f32),
        in_specs=[pl.BlockSpec(memory_space=pltpu.HBM)] * 5,
        out_specs=pl.BlockSpec(memory_space=pltpu.VMEM),
        scratch_shapes=[
            pltpu.VMEM((3, cells, rows + 2 * EDGE, width), f32),
            pltpu.VMEM((3, cells, rows, width), f32),
            pltpu.VMEM((2, cells, rows, width), f32),
            pltpu.VMEM((rows, width), f32),
            pltpu.VMEM((3, rows, width), f32),
            pltpu.VMEM((9, cells, rows, width), f32),
            pltpu.VMEM((3, cells, rows, width), f32),
            pltpu.VMEM((group, 9, part, width), f32),
            pltpu.VMEM((group, 9, part, width), f32),
            pltpu.VMEM((9, part, width), f32),
            pltpu.VMEM((groups, 9, part, width), f32),
            pltpu.VMEM((group, 3, part, width), f32),
            pltpu.VMEM((group, 3, part, width), f32),
            dma((3,)), dma((2, rows // max(part, EDGE))), dma((2,)), dma((2,)),
            dma((group,)), dma((group,)), dma((group,)), dma((group,)),
            dma((groups,)), dma((groups,)), dma((groups,)), dma((groups,)),
            dma((group,)), dma((group,)),
        ],
        compiler_params=pltpu.CompilerParams(
            collective_id=0, has_side_effects=True, vmem_limit_bytes=24 * 2**20
        ),
        cost_estimate=pl.CostEstimate(
            flops=100 * cells * rows * width, bytes_accessed=44 * cells * rows * width,
            transcendentals=0,
        ),
    )(*(
        pltpu.with_memory_space_constraint(array, pltpu.HBM)
        for array in (concentration, courant, rates, spread, inlet)
    ))


def solution(mesh):
    in_specs = (
        P(None, "flow", "lat", None),
        P(None, "flow", "lat", None),
        P(None, "flow", "lat", None),
        P("lat", None),
        P(None, "lat", None),
    )
    out_specs = P(None, "flow", "lat", None)
    body = functools.partial(per_device, mesh.shape["flow"], mesh.shape["lat"])
    return jax.shard_map(
        body, mesh=mesh, in_specs=in_specs, out_specs=out_specs, check_vma=False
    )
```

```python
import functools
import jax
import jax.numpy as jnp
from jax import lax
from jax.experimental import pallas as pl
from jax.experimental.pallas import tpu as pltpu
from jax.sharding import PartitionSpec as P

MESH = pl.DeviceIdType.MESH
GROUP = 4
EDGE = 8
UNROLL = 16


def apply_map(m, q):
    return (
        m[0] * q[0] + m[6],
        m[1] * q[0] + m[2] * q[1] + m[7],
        m[3] * q[0] + m[4] * q[1] + m[5] * q[2] + m[8],
    )


def times(m, n):
    return (
        m[0] * n[0],
        m[1] * n[0] + m[2] * n[1],
        m[2] * n[2],
        m[3] * n[0] + m[4] * n[1] + m[5] * n[3],
        m[4] * n[2] + m[5] * n[4],
        m[5] * n[5],
    )


def inverse(x):
    rough = pl.reciprocal(x, approx=True)
    return rough * (2.0 - x * rough)


def kernel(
    groups, group, lats,
    conc, courant, rates, spread, inlet, out,
    pad, cour, rate, spr, inl, local, inv, mine, maps, total, totals, fluxes, entering,
    load_sem, tile_sem, halo_send, halo_recv,
    a_send, a_recv, o_send, o_recv, b_send, b_recv, p_send, p_recv, c_send, c_recv,
):
    cells, rows, width = cour.shape[1:]
    part = rows // group
    tile = max(part, EDGE)
    owners = tile // part
    tiles = rows // tile
    flow = lax.axis_index("flow")
    lat = lax.axis_index("lat")
    inner = lax.rem(flow, group)
    outer = lax.div(flow, group)
    not_low, not_high = lat > 0, lat < lats - 1

    def tile_at(step):
        return lax.rem(lax.div(inner, owners) + step, tiles)

    def rows_of(t):
        return pl.ds(pl.multiple_of(t * tile, tile), tile)

    def nth(n):
        return tile_at(n + 1)

    def tile_loads(n):
        at = rows_of(nth(n))
        return (
            pltpu.make_async_copy(courant.at[:, :, at], cour.at[:, :, at], tile_sem.at[0, n]),
            pltpu.make_async_copy(rates.at[:, :, at], rate.at[:, :, at], tile_sem.at[1, n]),
        )

    loads = [
        pltpu.make_async_copy(src, dst, load_sem.at[i])
        for i, (src, dst) in enumerate((
            (conc, pad.at[:, :, EDGE:EDGE + rows]), (spread, spr), (inlet, inl),
        ))
    ]
    barrier = pltpu.get_barrier_semaphore()
    for step in range(1, group):
        peer = outer * group + lax.rem(inner + step, group)
        pl.semaphore_signal(barrier, inc=1, device_id={"flow": peer}, device_id_type=MESH)
    for step in range(1, groups):
        peer = lax.rem(outer + step, groups) * group + inner
        pl.semaphore_signal(barrier, inc=1, device_id={"flow": peer}, device_id_type=MESH)

    @pl.when(not_low)
    def _():
        pl.semaphore_signal(barrier, inc=1, device_id={"lat": lat - 1}, device_id_type=MESH)

    @pl.when(not_high)
    def _():
        pl.semaphore_signal(barrier, inc=1, device_id={"lat": lat + 1}, device_id_type=MESH)

    for n in range(tiles):
        for load in tile_loads(n):
            load.start()
    for load in loads:
        load.start()

    nothing = jnp.zeros((3, cells, EDGE, width), jnp.float32)

    @pl.when(lat == 0)
    def _():
        pad[:, :, 0:EDGE] = nothing

    @pl.when(lat == lats - 1)
    def _():
        pad[:, :, EDGE + rows:2 * EDGE + rows] = nothing

    beside = jnp.where(not_low, 1, 0) + jnp.where(not_high, 1, 0)
    pl.semaphore_wait(barrier, group - 1 + groups - 1 + beside)

    to_high = pltpu.make_async_remote_copy(
        src_ref=conc.at[:, :, rows - 1:rows], dst_ref=pad.at[:, :, EDGE - 1:EDGE],
        send_sem=halo_send.at[0], recv_sem=halo_recv.at[0],
        device_id={"lat": lat + 1}, device_id_type=MESH,
    )
    to_low = pltpu.make_async_remote_copy(
        src_ref=conc.at[:, :, 0:1], dst_ref=pad.at[:, :, EDGE + rows:EDGE + rows + 1],
        send_sem=halo_send.at[1], recv_sem=halo_recv.at[1],
        device_id={"lat": lat - 1}, device_id_type=MESH,
    )

    @pl.when(not_high)
    def _():
        to_high.start()

    @pl.when(not_low)
    def _():
        to_low.start()

    matrix, offset = slice(0, 6), slice(6, 9)

    def between(src, dst, there, send, recv, slot, cut, peer, arriving):
        lands = peer if arriving else slot
        return pltpu.make_async_remote_copy(
            src_ref=src.at[peer, cut], dst_ref=dst.at[lands, cut],
            send_sem=send.at[peer], recv_sem=recv.at[lands],
            device_id={"flow": there(peer)}, device_id_type=MESH,
        )

    def member(peer):
        return outer * group + peer

    def matrix_copy(peer, arriving=False):
        return between(mine, maps, member, a_send, a_recv, inner, matrix, peer, arriving)

    def offset_copy(peer, arriving=False):
        return between(mine, maps, member, o_send, o_recv, inner, offset, peer, arriving)

    def flux_copy(peer, arriving=False):
        return between(fluxes, entering, member, c_send, c_recv, inner, slice(0, 3), peer, arriving)

    def put(t, values, first, copy):
        for j in range(owners):
            peer = t * owners + j
            for q, value in enumerate(values):
                mine[peer, first + q] = value[j * part:(j + 1) * part]

            @pl.when(peer != inner)
            def _():
                copy(peer).start()

    one = jnp.ones((tile, width), jnp.float32)
    zero = jnp.zeros((tile, width), jnp.float32)

    def matrix_tile(n, carry):
        for load in tile_loads(n):
            load.wait()
        t = nth(n)
        at = rows_of(t)

        def matrix_cell(i, state):
            m00, m10, m11, m20, m21, m22 = state
            c0, c1, c2 = cour[0, i, at], cour[1, i, at], cour[2, i, at]
            k0, k1 = rate[0, i, at], rate[1, i, at]
            r0, r1, r2 = inverse(1.0 + c0 + k0), inverse(1.0 + c1 + k1), inverse(1.0 + c2)
            for k, r in enumerate((r0, r1, r2)):
                inv[k, i, at] = r
            u00 = m00 * r0
            u10 = (m10 + k0 * u00) * r1
            u20 = (m20 + k1 * u10) * r2
            u11 = m11 * r1
            u21 = (m21 + k1 * u11) * r2
            u22 = m22 * r2
            for q, value in enumerate((u00, u10, u11, u20, u21, u22)):
                local[q, i, at] = value
            return c0 * u00, c1 * u10, c1 * u11, c2 * u20, c2 * u21, c2 * u22

        state = lax.fori_loop(
            0, cells, matrix_cell, (one, zero, one, zero, zero, one), unroll=UNROLL
        )
        put(t, state, 0, matrix_copy)
        return carry

    lax.fori_loop(0, tiles, matrix_tile, 0)

    for load in loads:
        load.wait()

    lane = lax.broadcasted_iota(jnp.int32, (tile, width), 1)
    first, last = lane == 0, lane == width - 1

    def group_copy(o, cut, send, recv, arriving):
        lands = o if arriving else outer
        return pltpu.make_async_remote_copy(
            src_ref=total.at[cut], dst_ref=totals.at[lands, cut],
            send_sem=send.at[o], recv_sem=recv.at[lands],
            device_id={"flow": o * group + inner}, device_id_type=MESH,
        )

    def total_matrix(o, arriving=False):
        return group_copy(o, matrix, b_send, b_recv, arriving)

    def total_offset(o, arriving=False):
        return group_copy(o, offset, p_send, p_recv, arriving)

    peers = [lax.rem(inner + step, group) for step in range(1, group)]

    def fold_matrices():
        maps[inner, matrix] = mine[inner, matrix]
        for peer in peers:
            matrix_copy(peer, True).wait_recv()

        if groups > 2:
            @pl.when((outer > 0) & (outer < groups - 1))
            def _():
                product = tuple(maps[0, q] for q in range(6))
                for m in range(1, group):
                    product = times(tuple(maps[m, q] for q in range(6)), product)
                for q in range(6):
                    total[q] = product[q]
                for o in range(2, groups):
                    @pl.when(outer < o)
                    def _():
                        total_matrix(o).start()

    last_inside = tiles - 1 - jnp.where(not_low & not_high, 1, 0)

    def offset_tile(n, carry):
        @pl.when((n == last_inside) & not_low)
        def _():
            to_high.wait_recv()

        @pl.when((n == last_inside) & not_high)
        def _():
            to_low.wait_recv()

        t = lax.rem(n + jnp.where(not_low, 1, 0), tiles)
        at = rows_of(t)
        scale = spr[at]

        def source(k, i):
            mid = pad[k, i, pl.ds(pl.multiple_of(t * tile + EDGE, EDGE), tile)]
            left = jnp.where(first, 0.0, pltpu.roll(mid, 1, 1))
            right = jnp.where(last, 0.0, pltpu.roll(mid, width - 1, 1))
            up = pad[k, i, pl.ds(t * tile + EDGE - 1, tile)]
            down = pad[k, i, pl.ds(t * tile + EDGE + 1, tile)]
            return mid + scale * (up + down + left + right - 4.0 * mid)

        def offset_cell(i, state):
            w0, w1, w2 = state
            v0 = (source(0, i) + w0) * inv[0, i, at]
            v1 = (source(1, i) + w1 + rate[0, i, at] * v0) * inv[1, i, at]
            v2 = (source(2, i) + w2 + rate[1, i, at] * v1) * inv[2, i, at]
            for k, value in enumerate((v0, v1, v2)):
                local[6 + k, i, at] = value
            return cour[0, i, at] * v0, cour[1, i, at] * v1, cour[2, i, at] * v2

        state = lax.fori_loop(0, cells, offset_cell, (zero, zero, zero), unroll=UNROLL)
        put(t, state, 6, offset_copy)
        return carry

    lax.fori_loop(0, tiles, offset_tile, 0)
    fold_matrices()

    def map_of(ref, m):
        return tuple(ref[m, q] for q in range(9))

    maps[inner, offset] = mine[inner, offset]
    for peer in peers:
        offset_copy(peer, True).wait_recv()

    inflow = tuple(inl[k, pl.ds(pl.multiple_of(inner * part, part), part)] for k in range(3))
    if groups > 1:
        shift = tuple(jnp.where(outer == 0, value, 0.0) for value in inflow)
        for m in range(group):
            shift = apply_map(map_of(maps, m), shift)
        for k in range(3):
            total[6 + k] = shift[k]
        for o in range(1, groups):
            @pl.when(outer < o)
            def _():
                total_offset(o).start()

        @pl.when(outer > 0)
        def _():
            total_offset(0, True).wait_recv()

        def earlier(o, flux):
            total_matrix(o, True).wait_recv()
            total_offset(o, True).wait_recv()
            return apply_map(map_of(totals, o), flux)

        @pl.when(outer == 0)
        def _():
            for k in range(3):
                fluxes[0, k] = inflow[k]

        @pl.when(outer > 0)
        def _():
            flux = lax.fori_loop(1, outer, earlier, tuple(totals[0, 6 + k] for k in range(3)))
            for k in range(3):
                fluxes[0, k] = flux[k]
    else:
        for k in range(3):
            fluxes[0, k] = inflow[k]

    flux = tuple(fluxes[0, k] for k in range(3))
    for m in range(1, group):
        flux = apply_map(map_of(maps, m - 1), flux)
        for k in range(3):
            fluxes[m, k] = flux[k]
    for peer in peers:
        flux_copy(peer).start()
    entering[inner] = fluxes[inner]

    for peer in peers:
        matrix_copy(peer).wait_send()
        offset_copy(peer).wait_send()
    for o in range(1, groups):
        @pl.when(outer < o)
        def _():
            total_offset(o).wait_send()

        @pl.when((outer > 0) & (outer < o))
        def _():
            total_matrix(o).wait_send()

    @pl.when(not_high)
    def _():
        to_high.wait_send()

    @pl.when(not_low)
    def _():
        to_low.wait_send()

    def finish_tile(step, carry):
        t = tile_at(step)
        at = rows_of(t)
        for j in range(owners):
            peer = t * owners + j

            @pl.when(peer != inner)
            def _():
                flux_copy(peer, True).wait_recv()
        q = [
            jnp.concatenate([entering[t * owners + j, k] for j in range(owners)], axis=0)
            for k in range(3)
        ]

        def finish(i, carry):
            fresh = apply_map(tuple(local[n, i, at] for n in range(9)), q)
            for k in range(3):
                out[k, i, at] = fresh[k]
            return carry

        return lax.fori_loop(0, cells, finish, carry, unroll=UNROLL)

    lax.fori_loop(0, tiles, finish_tile, 0)

    for peer in peers:
        flux_copy(peer).wait_send()


def per_device(flows, lats, concentration, courant, rates, spread, inlet):
    _, cells, rows, width = concentration.shape
    group = GROUP
    groups = flows // group
    part = rows // group
    f32 = jnp.float32
    dma = pltpu.SemaphoreType.DMA
    return pl.pallas_call(
        functools.partial(kernel, groups, group, lats),
        out_shape=jax.ShapeDtypeStruct(concentration.shape, f32),
        in_specs=[pl.BlockSpec(memory_space=pltpu.HBM)] * 5,
        out_specs=pl.BlockSpec(memory_space=pltpu.VMEM),
        scratch_shapes=[
            pltpu.VMEM((3, cells, rows + 2 * EDGE, width), f32),
            pltpu.VMEM((3, cells, rows, width), f32),
            pltpu.VMEM((2, cells, rows, width), f32),
            pltpu.VMEM((rows, width), f32),
            pltpu.VMEM((3, rows, width), f32),
            pltpu.VMEM((9, cells, rows, width), f32),
            pltpu.VMEM((3, cells, rows, width), f32),
            pltpu.VMEM((group, 9, part, width), f32),
            pltpu.VMEM((group, 9, part, width), f32),
            pltpu.VMEM((9, part, width), f32),
            pltpu.VMEM((groups, 9, part, width), f32),
            pltpu.VMEM((group, 3, part, width), f32),
            pltpu.VMEM((group, 3, part, width), f32),
            dma((3,)), dma((2, rows // max(part, EDGE))), dma((2,)), dma((2,)),
            dma((group,)), dma((group,)), dma((group,)), dma((group,)),
            dma((groups,)), dma((groups,)), dma((groups,)), dma((groups,)),
            dma((group,)), dma((group,)),
        ],
        compiler_params=pltpu.CompilerParams(
            collective_id=0, has_side_effects=True, vmem_limit_bytes=24 * 2**20
        ),
        cost_estimate=pl.CostEstimate(
            flops=100 * cells * rows * width, bytes_accessed=44 * cells * rows * width,
            transcendentals=0,
        ),
    )(*(
        pltpu.with_memory_space_constraint(array, pltpu.HBM)
        for array in (concentration, courant, rates, spread, inlet)
    ))


def solution(mesh):
    in_specs = (
        P(None, "flow", "lat", None),
        P(None, "flow", "lat", None),
        P(None, "flow", "lat", None),
        P("lat", None),
        P(None, "lat", None),
    )
    out_specs = P(None, "flow", "lat", None)
    body = functools.partial(per_device, mesh.shape["flow"], mesh.shape["lat"])
    return jax.shard_map(
        body, mesh=mesh, in_specs=in_specs, out_specs=out_specs, check_vma=False
    )
```

```python
import functools
import jax
import jax.numpy as jnp
from jax import lax
from jax.experimental import pallas as pl
from jax.experimental.pallas import tpu as pltpu
from jax.sharding import PartitionSpec as P

MESH = pl.DeviceIdType.MESH
GROUP = 8
EDGE = 8
UNROLL = 16


def apply_map(m, q):
    return (
        m[0] * q[0] + m[6],
        m[1] * q[0] + m[2] * q[1] + m[7],
        m[3] * q[0] + m[4] * q[1] + m[5] * q[2] + m[8],
    )


def times(m, n):
    return (
        m[0] * n[0],
        m[1] * n[0] + m[2] * n[1],
        m[2] * n[2],
        m[3] * n[0] + m[4] * n[1] + m[5] * n[3],
        m[4] * n[2] + m[5] * n[4],
        m[5] * n[5],
    )


def inverse(x):
    rough = pl.reciprocal(x, approx=True)
    return rough * (2.0 - x * rough)


def kernel(
    groups, group, lats,
    conc, courant, rates, spread, inlet, out,
    pad, cour, rate, spr, inl, local, inv, mine, maps, total, totals, fluxes, entering,
    load_sem, tile_sem, halo_send, halo_recv,
    a_send, a_recv, o_send, o_recv, b_send, b_recv, p_send, p_recv, c_send, c_recv,
):
    cells, rows, width = cour.shape[1:]
    part = rows // group
    tile = max(part, EDGE)
    owners = tile // part
    tiles = rows // tile
    flow = lax.axis_index("flow")
    lat = lax.axis_index("lat")
    inner = lax.rem(flow, group)
    outer = lax.div(flow, group)
    not_low, not_high = lat > 0, lat < lats - 1

    def tile_at(step):
        return lax.rem(lax.div(inner, owners) + step, tiles)

    def rows_of(t):
        return pl.ds(pl.multiple_of(t * tile, tile), tile)

    def nth(n):
        return tile_at(n + 1)

    def tile_loads(n):
        at = rows_of(nth(n))
        return (
            pltpu.make_async_copy(courant.at[:, :, at], cour.at[:, :, at], tile_sem.at[0, n]),
            pltpu.make_async_copy(rates.at[:, :, at], rate.at[:, :, at], tile_sem.at[1, n]),
        )

    loads = [
        pltpu.make_async_copy(src, dst, load_sem.at[i])
        for i, (src, dst) in enumerate((
            (conc, pad.at[:, :, EDGE:EDGE + rows]), (spread, spr), (inlet, inl),
        ))
    ]
    barrier = pltpu.get_barrier_semaphore()
    for step in range(1, group):
        peer = outer * group + lax.rem(inner + step, group)
        pl.semaphore_signal(barrier, inc=1, device_id={"flow": peer}, device_id_type=MESH)
    for step in range(1, groups):
        peer = lax.rem(outer + step, groups) * group + inner
        pl.semaphore_signal(barrier, inc=1, device_id={"flow": peer}, device_id_type=MESH)

    @pl.when(not_low)
    def _():
        pl.semaphore_signal(barrier, inc=1, device_id={"lat": lat - 1}, device_id_type=MESH)

    @pl.when(not_high)
    def _():
        pl.semaphore_signal(barrier, inc=1, device_id={"lat": lat + 1}, device_id_type=MESH)

    for n in range(tiles):
        for load in tile_loads(n):
            load.start()
    for load in loads:
        load.start()

    nothing = jnp.zeros((3, cells, EDGE, width), jnp.float32)

    @pl.when(lat == 0)
    def _():
        pad[:, :, 0:EDGE] = nothing

    @pl.when(lat == lats - 1)
    def _():
        pad[:, :, EDGE + rows:2 * EDGE + rows] = nothing

    beside = jnp.where(not_low, 1, 0) + jnp.where(not_high, 1, 0)
    pl.semaphore_wait(barrier, group - 1 + groups - 1 + beside)

    to_high = pltpu.make_async_remote_copy(
        src_ref=conc.at[:, :, rows - 1:rows], dst_ref=pad.at[:, :, EDGE - 1:EDGE],
        send_sem=halo_send.at[0], recv_sem=halo_recv.at[0],
        device_id={"lat": lat + 1}, device_id_type=MESH,
    )
    to_low = pltpu.make_async_remote_copy(
        src_ref=conc.at[:, :, 0:1], dst_ref=pad.at[:, :, EDGE + rows:EDGE + rows + 1],
        send_sem=halo_send.at[1], recv_sem=halo_recv.at[1],
        device_id={"lat": lat - 1}, device_id_type=MESH,
    )

    @pl.when(not_high)
    def _():
        to_high.start()

    @pl.when(not_low)
    def _():
        to_low.start()

    matrix, offset = slice(0, 6), slice(6, 9)

    def between(src, dst, there, send, recv, slot, cut, peer, arriving):
        lands = peer if arriving else slot
        return pltpu.make_async_remote_copy(
            src_ref=src.at[peer, cut], dst_ref=dst.at[lands, cut],
            send_sem=send.at[peer], recv_sem=recv.at[lands],
            device_id={"flow": there(peer)}, device_id_type=MESH,
        )

    def member(peer):
        return outer * group + peer

    def matrix_copy(peer, arriving=False):
        return between(mine, maps, member, a_send, a_recv, inner, matrix, peer, arriving)

    def offset_copy(peer, arriving=False):
        return between(mine, maps, member, o_send, o_recv, inner, offset, peer, arriving)

    def flux_copy(peer, arriving=False):
        return between(fluxes, entering, member, c_send, c_recv, inner, slice(0, 3), peer, arriving)

    def put(t, values, first, copy):
        for j in range(owners):
            peer = t * owners + j
            for q, value in enumerate(values):
                mine[peer, first + q] = value[j * part:(j + 1) * part]

            @pl.when(peer != inner)
            def _():
                copy(peer).start()

    one = jnp.ones((tile, width), jnp.float32)
    zero = jnp.zeros((tile, width), jnp.float32)

    def matrix_tile(n, carry):
        for load in tile_loads(n):
            load.wait()
        t = nth(n)
        at = rows_of(t)

        def matrix_cell(i, state):
            m00, m10, m11, m20, m21, m22 = state
            c0, c1, c2 = cour[0, i, at], cour[1, i, at], cour[2, i, at]
            k0, k1 = rate[0, i, at], rate[1, i, at]
            r0, r1, r2 = inverse(1.0 + c0 + k0), inverse(1.0 + c1 + k1), inverse(1.0 + c2)
            for k, r in enumerate((r0, r1, r2)):
                inv[k, i, at] = r
            u00 = m00 * r0
            u10 = (m10 + k0 * u00) * r1
            u20 = (m20 + k1 * u10) * r2
            u11 = m11 * r1
            u21 = (m21 + k1 * u11) * r2
            u22 = m22 * r2
            for q, value in enumerate((u00, u10, u11, u20, u21, u22)):
                local[q, i, at] = value
            return c0 * u00, c1 * u10, c1 * u11, c2 * u20, c2 * u21, c2 * u22

        state = lax.fori_loop(
            0, cells, matrix_cell, (one, zero, one, zero, zero, one), unroll=UNROLL
        )
        put(t, state, 0, matrix_copy)
        return carry

    lax.fori_loop(0, tiles, matrix_tile, 0)

    for load in loads:
        load.wait()

    lane = lax.broadcasted_iota(jnp.int32, (tile, width), 1)
    first, last = lane == 0, lane == width - 1

    def group_copy(o, cut, send, recv, arriving):
        lands = o if arriving else outer
        return pltpu.make_async_remote_copy(
            src_ref=total.at[cut], dst_ref=totals.at[lands, cut],
            send_sem=send.at[o], recv_sem=recv.at[lands],
            device_id={"flow": o * group + inner}, device_id_type=MESH,
        )

    def total_matrix(o, arriving=False):
        return group_copy(o, matrix, b_send, b_recv, arriving)

    def total_offset(o, arriving=False):
        return group_copy(o, offset, p_send, p_recv, arriving)

    peers = [lax.rem(inner + step, group) for step in range(1, group)]

    def fold_matrices():
        maps[inner, matrix] = mine[inner, matrix]
        for peer in peers:
            matrix_copy(peer, True).wait_recv()

        if groups > 2:
            @pl.when((outer > 0) & (outer < groups - 1))
            def _():
                product = tuple(maps[0, q] for q in range(6))
                for m in range(1, group):
                    product = times(tuple(maps[m, q] for q in range(6)), product)
                for q in range(6):
                    total[q] = product[q]
                for o in range(2, groups):
                    @pl.when(outer < o)
                    def _():
                        total_matrix(o).start()

    last_inside = tiles - 1 - jnp.where(not_low & not_high, 1, 0)

    def offset_tile(n, carry):
        @pl.when((n == last_inside) & not_low)
        def _():
            to_high.wait_recv()

        @pl.when((n == last_inside) & not_high)
        def _():
            to_low.wait_recv()

        t = lax.rem(n + jnp.where(not_low, 1, 0), tiles)
        at = rows_of(t)
        scale = spr[at]

        def source(k, i):
            mid = pad[k, i, pl.ds(pl.multiple_of(t * tile + EDGE, EDGE), tile)]
            left = jnp.where(first, 0.0, pltpu.roll(mid, 1, 1))
            right = jnp.where(last, 0.0, pltpu.roll(mid, width - 1, 1))
            up = pad[k, i, pl.ds(t * tile + EDGE - 1, tile)]
            down = pad[k, i, pl.ds(t * tile + EDGE + 1, tile)]
            return mid + scale * (up + down + left + right - 4.0 * mid)

        def offset_cell(i, state):
            w0, w1, w2 = state
            v0 = (source(0, i) + w0) * inv[0, i, at]
            v1 = (source(1, i) + w1 + rate[0, i, at] * v0) * inv[1, i, at]
            v2 = (source(2, i) + w2 + rate[1, i, at] * v1) * inv[2, i, at]
            for k, value in enumerate((v0, v1, v2)):
                local[6 + k, i, at] = value
            return cour[0, i, at] * v0, cour[1, i, at] * v1, cour[2, i, at] * v2

        state = lax.fori_loop(0, cells, offset_cell, (zero, zero, zero), unroll=UNROLL)
        put(t, state, 6, offset_copy)
        return carry

    lax.fori_loop(0, tiles, offset_tile, 0)
    fold_matrices()

    def map_of(ref, m):
        return tuple(ref[m, q] for q in range(9))

    maps[inner, offset] = mine[inner, offset]
    for peer in peers:
        offset_copy(peer, True).wait_recv()

    inflow = tuple(inl[k, pl.ds(pl.multiple_of(inner * part, part), part)] for k in range(3))
    if groups > 1:
        shift = tuple(jnp.where(outer == 0, value, 0.0) for value in inflow)
        for m in range(group):
            shift = apply_map(map_of(maps, m), shift)
        for k in range(3):
            total[6 + k] = shift[k]
        for o in range(1, groups):
            @pl.when(outer < o)
            def _():
                total_offset(o).start()

        @pl.when(outer > 0)
        def _():
            total_offset(0, True).wait_recv()

        def earlier(o, flux):
            total_matrix(o, True).wait_recv()
            total_offset(o, True).wait_recv()
            return apply_map(map_of(totals, o), flux)

        @pl.when(outer == 0)
        def _():
            for k in range(3):
                fluxes[0, k] = inflow[k]

        @pl.when(outer > 0)
        def _():
            flux = lax.fori_loop(1, outer, earlier, tuple(totals[0, 6 + k] for k in range(3)))
            for k in range(3):
                fluxes[0, k] = flux[k]
    else:
        for k in range(3):
            fluxes[0, k] = inflow[k]

    flux = tuple(fluxes[0, k] for k in range(3))
    for m in range(1, group):
        flux = apply_map(map_of(maps, m - 1), flux)
        for k in range(3):
            fluxes[m, k] = flux[k]
    for peer in peers:
        flux_copy(peer).start()
    entering[inner] = fluxes[inner]

    for peer in peers:
        matrix_copy(peer).wait_send()
        offset_copy(peer).wait_send()
    for o in range(1, groups):
        @pl.when(outer < o)
        def _():
            total_offset(o).wait_send()

        @pl.when((outer > 0) & (outer < o))
        def _():
            total_matrix(o).wait_send()

    @pl.when(not_high)
    def _():
        to_high.wait_send()

    @pl.when(not_low)
    def _():
        to_low.wait_send()

    def finish_tile(step, carry):
        t = tile_at(step)
        at = rows_of(t)
        for j in range(owners):
            peer = t * owners + j

            @pl.when(peer != inner)
            def _():
                flux_copy(peer, True).wait_recv()
        q = [
            jnp.concatenate([entering[t * owners + j, k] for j in range(owners)], axis=0)
            for k in range(3)
        ]

        def finish(i, carry):
            fresh = apply_map(tuple(local[n, i, at] for n in range(9)), q)
            for k in range(3):
                out[k, i, at] = fresh[k]
            return carry

        return lax.fori_loop(0, cells, finish, carry, unroll=UNROLL)

    lax.fori_loop(0, tiles, finish_tile, 0)

    for peer in peers:
        flux_copy(peer).wait_send()


def per_device(flows, lats, concentration, courant, rates, spread, inlet):
    _, cells, rows, width = concentration.shape
    group = GROUP
    groups = flows // group
    part = rows // group
    f32 = jnp.float32
    dma = pltpu.SemaphoreType.DMA
    return pl.pallas_call(
        functools.partial(kernel, groups, group, lats),
        out_shape=jax.ShapeDtypeStruct(concentration.shape, f32),
        in_specs=[pl.BlockSpec(memory_space=pltpu.HBM)] * 5,
        out_specs=pl.BlockSpec(memory_space=pltpu.VMEM),
        scratch_shapes=[
            pltpu.VMEM((3, cells, rows + 2 * EDGE, width), f32),
            pltpu.VMEM((3, cells, rows, width), f32),
            pltpu.VMEM((2, cells, rows, width), f32),
            pltpu.VMEM((rows, width), f32),
            pltpu.VMEM((3, rows, width), f32),
            pltpu.VMEM((9, cells, rows, width), f32),
            pltpu.VMEM((3, cells, rows, width), f32),
            pltpu.VMEM((group, 9, part, width), f32),
            pltpu.VMEM((group, 9, part, width), f32),
            pltpu.VMEM((9, part, width), f32),
            pltpu.VMEM((groups, 9, part, width), f32),
            pltpu.VMEM((group, 3, part, width), f32),
            pltpu.VMEM((group, 3, part, width), f32),
            dma((3,)), dma((2, rows // max(part, EDGE))), dma((2,)), dma((2,)),
            dma((group,)), dma((group,)), dma((group,)), dma((group,)),
            dma((groups,)), dma((groups,)), dma((groups,)), dma((groups,)),
            dma((group,)), dma((group,)),
        ],
        compiler_params=pltpu.CompilerParams(
            collective_id=0, has_side_effects=True, vmem_limit_bytes=24 * 2**20
        ),
        cost_estimate=pl.CostEstimate(
            flops=100 * cells * rows * width, bytes_accessed=44 * cells * rows * width,
            transcendentals=0,
        ),
    )(*(
        pltpu.with_memory_space_constraint(array, pltpu.HBM)
        for array in (concentration, courant, rates, spread, inlet)
    ))


def solution(mesh):
    in_specs = (
        P(None, "flow", "lat", None),
        P(None, "flow", "lat", None),
        P(None, "flow", "lat", None),
        P("lat", None),
        P(None, "lat", None),
    )
    out_specs = P(None, "flow", "lat", None)
    body = functools.partial(per_device, mesh.shape["flow"], mesh.shape["lat"])
    return jax.shard_map(
        body, mesh=mesh, in_specs=in_specs, out_specs=out_specs, check_vma=False
    )
```

```python
import functools
import jax
import jax.numpy as jnp
from jax import lax
from jax.experimental import pallas as pl
from jax.experimental.pallas import tpu as pltpu
from jax.sharding import PartitionSpec as P

MESH = pl.DeviceIdType.MESH
GROUP = 4
EDGE = 8
UNROLL = 16


def apply_map(m, q):
    return (
        m[0] * q[0] + m[6],
        m[1] * q[0] + m[2] * q[1] + m[7],
        m[3] * q[0] + m[4] * q[1] + m[5] * q[2] + m[8],
    )


def times(m, n):
    return (
        m[0] * n[0],
        m[1] * n[0] + m[2] * n[1],
        m[2] * n[2],
        m[3] * n[0] + m[4] * n[1] + m[5] * n[3],
        m[4] * n[2] + m[5] * n[4],
        m[5] * n[5],
    )


def inverse(x):
    rough = pl.reciprocal(x, approx=True)
    return rough * (2.0 - x * rough)


def kernel(
    groups, group, lats,
    conc, courant, rates, spread, inlet, out,
    pad, cour, rate, spr, inl, local, inv, mine, maps, total, totals, fluxes, entering,
    load_sem, tile_sem, halo_send, halo_recv,
    a_send, a_recv, o_send, o_recv, b_send, b_recv, p_send, p_recv, c_send, c_recv,
):
    cells, rows, width = cour.shape[1:]
    part = rows // group
    tile = max(part, EDGE)
    owners = tile // part
    tiles = rows // tile
    flow = lax.axis_index("flow")
    lat = lax.axis_index("lat")
    inner = lax.rem(flow, group)
    outer = lax.div(flow, group)
    not_low, not_high = lat > 0, lat < lats - 1

    def tile_at(step):
        return lax.rem(lax.div(inner, owners) + step, tiles)

    def rows_of(t):
        return pl.ds(pl.multiple_of(t * tile, tile), tile)

    def nth(n):
        return tile_at(n + 1)

    def tile_loads(n):
        at = rows_of(nth(n))
        return (
            pltpu.make_async_copy(courant.at[:, :, at], cour.at[:, :, at], tile_sem.at[0, n]),
            pltpu.make_async_copy(rates.at[:, :, at], rate.at[:, :, at], tile_sem.at[1, n]),
        )

    loads = [
        pltpu.make_async_copy(src, dst, load_sem.at[i])
        for i, (src, dst) in enumerate((
            (conc, pad.at[:, :, EDGE:EDGE + rows]), (spread, spr), (inlet, inl),
        ))
    ]
    barrier = pltpu.get_barrier_semaphore()
    for step in range(1, group):
        peer = outer * group + lax.rem(inner + step, group)
        pl.semaphore_signal(barrier, inc=1, device_id={"flow": peer}, device_id_type=MESH)
    for o in range(groups - 1):
        @pl.when(o < outer)
        def _():
            pl.semaphore_signal(
                barrier, inc=1, device_id={"flow": o * group + inner}, device_id_type=MESH
            )

    @pl.when(not_low)
    def _():
        pl.semaphore_signal(barrier, inc=1, device_id={"lat": lat - 1}, device_id_type=MESH)

    @pl.when(not_high)
    def _():
        pl.semaphore_signal(barrier, inc=1, device_id={"lat": lat + 1}, device_id_type=MESH)

    for n in range(tiles):
        for load in tile_loads(n):
            load.start()
    for load in loads:
        load.start()

    nothing = jnp.zeros((3, cells, EDGE, width), jnp.float32)

    @pl.when(lat == 0)
    def _():
        pad[:, :, 0:EDGE] = nothing

    @pl.when(lat == lats - 1)
    def _():
        pad[:, :, EDGE + rows:2 * EDGE + rows] = nothing

    beside = jnp.where(not_low, 1, 0) + jnp.where(not_high, 1, 0)
    pl.semaphore_wait(barrier, group - 1 + groups - 1 - outer + beside)

    to_high = pltpu.make_async_remote_copy(
        src_ref=conc.at[:, :, rows - 1:rows], dst_ref=pad.at[:, :, EDGE - 1:EDGE],
        send_sem=halo_send.at[0], recv_sem=halo_recv.at[0],
        device_id={"lat": lat + 1}, device_id_type=MESH,
    )
    to_low = pltpu.make_async_remote_copy(
        src_ref=conc.at[:, :, 0:1], dst_ref=pad.at[:, :, EDGE + rows:EDGE + rows + 1],
        send_sem=halo_send.at[1], recv_sem=halo_recv.at[1],
        device_id={"lat": lat - 1}, device_id_type=MESH,
    )

    @pl.when(not_high)
    def _():
        to_high.start()

    @pl.when(not_low)
    def _():
        to_low.start()

    matrix, offset = slice(0, 6), slice(6, 9)

    def between(src, dst, there, send, recv, slot, cut, peer, arriving):
        lands = peer if arriving else slot
        return pltpu.make_async_remote_copy(
            src_ref=src.at[peer, cut], dst_ref=dst.at[lands, cut],
            send_sem=send.at[peer], recv_sem=recv.at[lands],
            device_id={"flow": there(peer)}, device_id_type=MESH,
        )

    def member(peer):
        return outer * group + peer

    def matrix_copy(peer, arriving=False):
        return between(mine, maps, member, a_send, a_recv, inner, matrix, peer, arriving)

    def offset_copy(peer, arriving=False):
        return between(mine, maps, member, o_send, o_recv, inner, offset, peer, arriving)

    def flux_copy(peer, arriving=False):
        return between(fluxes, entering, member, c_send, c_recv, inner, slice(0, 3), peer, arriving)

    def put(t, values, first, copy):
        for j in range(owners):
            peer = t * owners + j
            for q, value in enumerate(values):
                mine[peer, first + q] = value[j * part:(j + 1) * part]

            @pl.when(peer != inner)
            def _():
                copy(peer).start()

    one = jnp.ones((tile, width), jnp.float32)
    zero = jnp.zeros((tile, width), jnp.float32)

    def matrix_tile(n, carry):
        for load in tile_loads(n):
            load.wait()
        t = nth(n)
        at = rows_of(t)

        def matrix_cell(i, state):
            m00, m10, m11, m20, m21, m22 = state
            c0, c1, c2 = cour[0, i, at], cour[1, i, at], cour[2, i, at]
            k0, k1 = rate[0, i, at], rate[1, i, at]
            r0, r1, r2 = inverse(1.0 + c0 + k0), inverse(1.0 + c1 + k1), inverse(1.0 + c2)
            for k, r in enumerate((r0, r1, r2)):
                inv[k, i, at] = r
            u00 = m00 * r0
            u10 = (m10 + k0 * u00) * r1
            u20 = (m20 + k1 * u10) * r2
            u11 = m11 * r1
            u21 = (m21 + k1 * u11) * r2
            u22 = m22 * r2
            for q, value in enumerate((u00, u10, u11, u20, u21, u22)):
                local[q, i, at] = value
            return c0 * u00, c1 * u10, c1 * u11, c2 * u20, c2 * u21, c2 * u22

        state = lax.fori_loop(
            0, cells, matrix_cell, (one, zero, one, zero, zero, one), unroll=UNROLL
        )
        put(t, state, 0, matrix_copy)
        return carry

    lax.fori_loop(0, tiles, matrix_tile, 0)

    for load in loads:
        load.wait()

    lane = lax.broadcasted_iota(jnp.int32, (tile, width), 1)
    first, last = lane == 0, lane == width - 1

    def group_copy(o, cut, send, recv, arriving):
        lands = o if arriving else outer
        return pltpu.make_async_remote_copy(
            src_ref=total.at[cut], dst_ref=totals.at[lands, cut],
            send_sem=send.at[o], recv_sem=recv.at[lands],
            device_id={"flow": o * group + inner}, device_id_type=MESH,
        )

    def total_matrix(o, arriving=False):
        return group_copy(o, matrix, b_send, b_recv, arriving)

    def total_offset(o, arriving=False):
        return group_copy(o, offset, p_send, p_recv, arriving)

    peers = [lax.rem(inner + step, group) for step in range(1, group)]

    def fold_matrices():
        maps[inner, matrix] = mine[inner, matrix]
        for peer in peers:
            matrix_copy(peer, True).wait_recv()

        if groups > 2:
            @pl.when((outer > 0) & (outer < groups - 1))
            def _():
                product = tuple(maps[0, q] for q in range(6))
                for m in range(1, group):
                    product = times(tuple(maps[m, q] for q in range(6)), product)
                for q in range(6):
                    total[q] = product[q]
                for o in range(2, groups):
                    @pl.when(outer < o)
                    def _():
                        total_matrix(o).start()

    last_inside = tiles - 1 - jnp.where(not_low & not_high, 1, 0)

    def offset_tile(n, carry):
        @pl.when((n == last_inside) & not_low)
        def _():
            to_high.wait_recv()

        @pl.when((n == last_inside) & not_high)
        def _():
            to_low.wait_recv()

        t = lax.rem(n + jnp.where(not_low, 1, 0), tiles)
        at = rows_of(t)
        scale = spr[at]

        def source(k, i):
            mid = pad[k, i, pl.ds(pl.multiple_of(t * tile + EDGE, EDGE), tile)]
            left = jnp.where(first, 0.0, pltpu.roll(mid, 1, 1))
            right = jnp.where(last, 0.0, pltpu.roll(mid, width - 1, 1))
            up = pad[k, i, pl.ds(t * tile + EDGE - 1, tile)]
            down = pad[k, i, pl.ds(t * tile + EDGE + 1, tile)]
            return mid + scale * (up + down + left + right - 4.0 * mid)

        def offset_cell(i, state):
            w0, w1, w2 = state
            v0 = (source(0, i) + w0) * inv[0, i, at]
            v1 = (source(1, i) + w1 + rate[0, i, at] * v0) * inv[1, i, at]
            v2 = (source(2, i) + w2 + rate[1, i, at] * v1) * inv[2, i, at]
            for k, value in enumerate((v0, v1, v2)):
                local[6 + k, i, at] = value
            return cour[0, i, at] * v0, cour[1, i, at] * v1, cour[2, i, at] * v2

        state = lax.fori_loop(0, cells, offset_cell, (zero, zero, zero), unroll=UNROLL)
        put(t, state, 6, offset_copy)
        return carry

    lax.fori_loop(0, tiles, offset_tile, 0)
    fold_matrices()

    def map_of(ref, m):
        return tuple(ref[m, q] for q in range(9))

    maps[inner, offset] = mine[inner, offset]
    for peer in peers:
        offset_copy(peer, True).wait_recv()

    inflow = tuple(inl[k, pl.ds(pl.multiple_of(inner * part, part), part)] for k in range(3))
    if groups > 1:
        shift = tuple(jnp.where(outer == 0, value, 0.0) for value in inflow)
        for m in range(group):
            shift = apply_map(map_of(maps, m), shift)
        for k in range(3):
            total[6 + k] = shift[k]
        for o in range(1, groups):
            @pl.when(outer < o)
            def _():
                total_offset(o).start()

        @pl.when(outer > 0)
        def _():
            total_offset(0, True).wait_recv()

        def earlier(o, flux):
            total_matrix(o, True).wait_recv()
            total_offset(o, True).wait_recv()
            return apply_map(map_of(totals, o), flux)

        @pl.when(outer == 0)
        def _():
            for k in range(3):
                fluxes[0, k] = inflow[k]

        @pl.when(outer > 0)
        def _():
            flux = lax.fori_loop(1, outer, earlier, tuple(totals[0, 6 + k] for k in range(3)))
            for k in range(3):
                fluxes[0, k] = flux[k]
    else:
        for k in range(3):
            fluxes[0, k] = inflow[k]

    flux = tuple(fluxes[0, k] for k in range(3))
    for m in range(1, group):
        flux = apply_map(map_of(maps, m - 1), flux)
        for k in range(3):
            fluxes[m, k] = flux[k]
    for peer in peers:
        flux_copy(peer).start()
    entering[inner] = fluxes[inner]

    for peer in peers:
        matrix_copy(peer).wait_send()
        offset_copy(peer).wait_send()
    for o in range(1, groups):
        @pl.when(outer < o)
        def _():
            total_offset(o).wait_send()

        @pl.when((outer > 0) & (outer < o))
        def _():
            total_matrix(o).wait_send()

    @pl.when(not_high)
    def _():
        to_high.wait_send()

    @pl.when(not_low)
    def _():
        to_low.wait_send()

    def finish_tile(step, carry):
        t = tile_at(step)
        at = rows_of(t)
        for j in range(owners):
            peer = t * owners + j

            @pl.when(peer != inner)
            def _():
                flux_copy(peer, True).wait_recv()
        q = [
            jnp.concatenate([entering[t * owners + j, k] for j in range(owners)], axis=0)
            for k in range(3)
        ]

        def finish(i, carry):
            fresh = apply_map(tuple(local[n, i, at] for n in range(9)), q)
            for k in range(3):
                out[k, i, at] = fresh[k]
            return carry

        return lax.fori_loop(0, cells, finish, carry, unroll=UNROLL)

    lax.fori_loop(0, tiles, finish_tile, 0)

    for peer in peers:
        flux_copy(peer).wait_send()


def per_device(flows, lats, concentration, courant, rates, spread, inlet):
    _, cells, rows, width = concentration.shape
    group = GROUP
    groups = flows // group
    part = rows // group
    f32 = jnp.float32
    dma = pltpu.SemaphoreType.DMA
    return pl.pallas_call(
        functools.partial(kernel, groups, group, lats),
        out_shape=jax.ShapeDtypeStruct(concentration.shape, f32),
        in_specs=[pl.BlockSpec(memory_space=pltpu.HBM)] * 5,
        out_specs=pl.BlockSpec(memory_space=pltpu.VMEM),
        scratch_shapes=[
            pltpu.VMEM((3, cells, rows + 2 * EDGE, width), f32),
            pltpu.VMEM((3, cells, rows, width), f32),
            pltpu.VMEM((2, cells, rows, width), f32),
            pltpu.VMEM((rows, width), f32),
            pltpu.VMEM((3, rows, width), f32),
            pltpu.VMEM((9, cells, rows, width), f32),
            pltpu.VMEM((3, cells, rows, width), f32),
            pltpu.VMEM((group, 9, part, width), f32),
            pltpu.VMEM((group, 9, part, width), f32),
            pltpu.VMEM((9, part, width), f32),
            pltpu.VMEM((groups, 9, part, width), f32),
            pltpu.VMEM((group, 3, part, width), f32),
            pltpu.VMEM((group, 3, part, width), f32),
            dma((3,)), dma((2, rows // max(part, EDGE))), dma((2,)), dma((2,)),
            dma((group,)), dma((group,)), dma((group,)), dma((group,)),
            dma((groups,)), dma((groups,)), dma((groups,)), dma((groups,)),
            dma((group,)), dma((group,)),
        ],
        compiler_params=pltpu.CompilerParams(
            collective_id=0, has_side_effects=True, vmem_limit_bytes=24 * 2**20
        ),
        cost_estimate=pl.CostEstimate(
            flops=100 * cells * rows * width, bytes_accessed=44 * cells * rows * width,
            transcendentals=0,
        ),
    )(*(
        pltpu.with_memory_space_constraint(array, pltpu.HBM)
        for array in (concentration, courant, rates, spread, inlet)
    ))


def solution(mesh):
    in_specs = (
        P(None, "flow", "lat", None),
        P(None, "flow", "lat", None),
        P(None, "flow", "lat", None),
        P("lat", None),
        P(None, "lat", None),
    )
    out_specs = P(None, "flow", "lat", None)
    body = functools.partial(per_device, mesh.shape["flow"], mesh.shape["lat"])
    return jax.shard_map(
        body, mesh=mesh, in_specs=in_specs, out_specs=out_specs, check_vma=False
    )
```
